32 devices in a mesh: pb: 8 (over y, x, core), pa: 4 (over z).
Axes of the slice: x: 2, y: 2, z: 4, core: 2. Of those that a mesh axis runs over, the one named last changes fastest.
Arguments:
- query_kv: bfloat16 [32, 2, 32, 1024], P(('pb', 'pa')), may hold values from -20 to 20
- student_query: bfloat16 [32, 1024], P(('pb', 'pa')), may hold values from -6 to 6
- block_holder: int32 [32, 2, 1], P('pb'), may hold values from 0 to 3; in each aligned block of 8 rows (0 to 7, 8 to 15, ..., all dimensions but the last counted through in order) at most 4 rows name the same one
- cand_local: int32 [32, 2, 32], P('pb'), may hold values from 0 to 63, all different within a row
- counts: int32 [32], P('pb'), may hold values from 1 to 64
- passage_qkv: bfloat16 [256, 3, 32, 1024], P(('pa', 'pb')), may hold values from -20 to 20
- passage_resid: bfloat16 [256, 1024], P(('pa', 'pb')), may hold values from -6 to 6
- student_passage: bfloat16 [256, 1024], P(('pa', 'pb')), may hold values from -6 to 6
- w_o: bfloat16 [1024, 1024], replicated, may hold values from -0.1875 to 0.1875
- ln_gain: float32 [1024], replicated, may hold values from 0.5 to 1.5
- ln_bias: float32 [1024], replicated, may hold values from -3 to 3
- w_dense: bfloat16 [1024, 1024], replicated, may hold values from -0.1875 to 0.1875
- b_dense: float32 [1024], replicated, may hold values from -3 to 3
- w_out: float32 [1024], replicated, may hold values from -0.6 to 0.6
Outputs:
- teacher_scores: float32 [32, 64], P(('pb', 'pa'))
- query_loss: float32 [32], P(('pb', 'pa'))
- grad_query: float32 [32, 1024], P(('pb', 'pa'))
- grad_passage: float32 [256, 1024], P(('pa', 'pb'))
The draws below stay inside these ranges and needn't reach their ends.
Inputs may be any that keep to these rules, and one draw needn't show every extreme that they name: `block_holder`: among the 8 candidate blocks of the queries of one index of pb, padding blocks included, no holder is named more than 4 times; in some index of pb one holder is named exactly 4 times. `cand_local`: the 32 entries of one block are distinct. Slots from counts[q] on are padding.
All inputs are finite; a program needn't handle non-finite values.
Results may differ from the reference program's by a relative error of at most 0.0038.
Values may be sent and summed in bfloat16 or wider, within the bound.
A program may use at most 128 MiB of HBM per device.

```python
import math
import jax
import jax.numpy as jnp
import numpy as np
from jax import lax

D = 1024
HEADS = 16
Q_LEN = 32
P_LEN = 32
BLOCK = 32
CAND_BLOCKS = 2
P_DEV = 8
HOLD_CAP = 4
POOL = 64
ROW_BLOCKS = 8
QUERIES = 32
PASSAGES = 256
N_PA = 4


def draw_query_kv(key, part):
    shape = (QUERIES, 2, Q_LEN, D)
    base = jnp.clip(jax.random.normal(jax.random.fold_in(key, 13), shape, jnp.float32), -5.0, 5.0)
    return base.astype(jnp.bfloat16)


def draw_passage_qkv(key, part):
    shape = (PASSAGES, 3, P_LEN, D)
    base = jnp.clip(jax.random.normal(jax.random.fold_in(key, 24), shape, jnp.float32), -5.0, 5.0)
    return base.astype(jnp.bfloat16)


def student_rows(key, salt, count):
    rows = jnp.clip(jax.random.normal(jax.random.fold_in(key, salt + 2), (count, D), jnp.float32), -5.0, 5.0)
    return rows.astype(jnp.bfloat16)


def draw_student_query(key, part):
    return student_rows(key, 31, QUERIES)


def draw_student_passage(key, part):
    return student_rows(key, 41, PASSAGES)


def set_ends(values, key, low, top_value):
    index_at = [jax.random.randint(jax.random.fold_in(key, axis), (), 0, length) for axis, length in enumerate(values.shape)]
    main_axis = values.shape.index(max(values.shape))
    beside = index_at[:main_axis] + [(index_at[main_axis] + 1) % values.shape[main_axis]] + index_at[main_axis + 1:]
    return values.at[tuple(index_at)].set(low).at[tuple(beside)].set(top_value)


def steps_of(own_key, dims, split, smallest, top_value):
    def one(position, shards_of):
        heights = jax.random.uniform(jax.random.fold_in(jax.random.fold_in(own_key, 6), position), (shards_of,), jnp.float32, smallest / len(split), top_value / len(split))
        return jnp.repeat(jnp.exp(heights), dims[position] // shards_of).reshape((-1,) + (1,) * (len(dims) - position - 1))

    loudness = one(*split[0])
    for cut in split[1:]:
        loudness = loudness * one(*cut)
    return loudness


def choose_distinct(key, rows, count, top, lift):
    ranking = jax.random.permutation(jax.random.fold_in(key, 1), count)
    boost = ranking
    for power in range(3):
        boost = boost * boost // count
    boost = boost * lift // count
    lots = jax.random.randint(jax.random.fold_in(key, 2), (rows, count), 0, 4096) + boost
    sure = jax.random.permutation(jax.random.fold_in(key, 3), rows)[jnp.arange(count) % rows]
    lots = jnp.where(jnp.arange(rows)[:, None] == sure[None, :], 1 << 14, lots)
    priority = lots * count + jnp.arange(count)
    return lax.top_k(priority.astype(jnp.int32), top)[1].astype(jnp.int32)


def deal_out(key, own, number, rows, number_of, top, most, lean):
    ranking = jax.random.permutation(key, number_of)
    packed, ordinary = load_shares(number_of, rows * top, most, lean, True), load_shares(number_of, rows * top, most, lean, False)
    places = jnp.arange(number_of)

    def named(tallies, turn):
        used = int((tallies > 0).sum())
        fixed = max(1, used // 4)
        passed = fixed + (places - fixed + turn * (used - fixed)) % max(1, number_of - fixed)
        return jnp.zeros((number_of,), jnp.int32).at[ranking[jnp.where(places < fixed, places, passed)]].set(jnp.asarray(tallies, jnp.int32))

    tallies = jnp.where(number % 4 == 0, named(packed, number // 4), named(ordinary, number - number // 4 - 1))
    mixed = jax.random.permutation(jax.random.fold_in(own, 3), number_of)
    giver, taker = mixed[0:number_of // 2 * 2:2], mixed[1:number_of // 2 * 2:2]
    room = jnp.minimum(tallies[giver] - 1, most - tallies[taker]) // 2
    room = jnp.where((giver == ranking[0]) | (taker == ranking[0]) | (tallies[taker] == 0), 0, jnp.maximum(room, 0))
    passed = jax.random.randint(jax.random.fold_in(own, 4), (number_of // 2,), 0, 1 << 20) % (room + 1)
    tallies = tallies.at[giver].add(-passed).at[taker].add(passed)
    members = jnp.searchsorted(jnp.cumsum(tallies), jnp.arange(rows * top), side="right").astype(jnp.int32)
    table = members.reshape(top, rows).T
    table = table[jax.random.permutation(jax.random.fold_in(own, 1), rows)]
    turn = jax.random.randint(jax.random.fold_in(own, 2), (rows, 1), 0, top)
    return jnp.take_along_axis(table, (jnp.arange(top)[None, :] + turn) % top, axis=1)


def load_shares(number_of, total, limit, lean, full):
    weights = [(1 << 20) // math.isqrt(grade ** lean) + 1 for grade in range(1, number_of + 1)]
    largest = limit if full else min(limit, max(-(-total // number_of), total * weights[0] // sum(weights)))
    least = 1 if total - largest >= number_of - 1 else 0
    given, surplus = [largest] + [least] * (number_of - 1), total - largest - least * (number_of - 1)
    while surplus > 0:
        movable = [i for i in range(1, number_of) if given[i] < largest] or [i for i in range(1, number_of) if given[i] < limit]
        pool, budget = sum([weights[i] for i in movable]), surplus
        for i in movable:
            more = min(limit - given[i], max(1, budget * weights[i] // pool), surplus)
            given[i] = given[i] + more
            surplus = surplus - more
    return np.array(given)


def centred(own_key, shape, scale, reach, cuts=(), held_as=jnp.bfloat16):
    array = jax.random.normal(own_key, shape, jnp.float32) * scale
    if len(cuts) > 0:
        array = steps_of(own_key, shape, cuts, -0.22, 0.18) * array
    return jnp.clip(array, min=-reach, max=reach).astype(held_as)


def setup_inputs(seed: int = 0) -> dict:
    splits = jax.random.split(jax.random.key(seed), 15)
    query_kv = draw_query_kv(jax.random.fold_in(splits[14], 71), 0)
    student_query = draw_student_query(jax.random.fold_in(splits[14], 71), 0)
    block_holder_keys = jax.random.split(jax.random.fold_in(splits[2], 1), QUERIES * CAND_BLOCKS // ROW_BLOCKS)
    block_holder_turns = jax.random.permutation(jax.random.fold_in(splits[2], 3), QUERIES * CAND_BLOCKS // ROW_BLOCKS)
    block_holder = jax.vmap(lambda own, number: deal_out(jax.random.fold_in(splits[2], 2), own, number, ROW_BLOCKS, N_PA, 1, HOLD_CAP, 1))(block_holder_keys, block_holder_turns).reshape((QUERIES, CAND_BLOCKS, 1))
    cand_local = choose_distinct(splits[3], QUERIES * CAND_BLOCKS, POOL, BLOCK, 0).reshape((QUERIES, CAND_BLOCKS, BLOCK))
    counts = set_ends(jax.random.randint(splits[4], (QUERIES,), 1, CAND_BLOCKS * BLOCK + 1), jax.random.fold_in(splits[4], 1), 1, CAND_BLOCKS * BLOCK).astype(jnp.int32)
    passage_qkv = draw_passage_qkv(jax.random.fold_in(splits[14], 71), 0)
    passage_resid = centred(splits[6], (PASSAGES, D), 1.0, 6.0, ((0, 32),))
    student_passage = draw_student_passage(jax.random.fold_in(splits[14], 71), 0)
    w_o = centred(splits[8], (D, D), D ** -0.5, 0.1875)
    ln_gain = jnp.clip(1.0 + 0.1 * jax.random.normal(splits[9], (D,), jnp.float32), 0.5, 1.5)
    ln_bias = centred(splits[10], (D,), 0.5, 3.0, (), jnp.float32)
    w_dense = centred(splits[11], (D, D), D ** -0.5, 0.1875)
    b_dense = centred(splits[12], (D,), 0.5, 3.0, (), jnp.float32)
    w_out = centred(splits[13], (D,), 0.1, 0.6, (), jnp.float32)
    return dict(query_kv=query_kv, student_query=student_query, block_holder=block_holder, cand_local=cand_local, counts=counts, passage_qkv=passage_qkv, passage_resid=passage_resid, student_passage=student_passage, w_o=w_o, ln_gain=ln_gain, ln_bias=ln_bias, w_dense=w_dense, b_dense=b_dense, w_out=w_out)


student_scale = 0.125
norm_eps = 1e-05

def self_attend(block_qkv):
    passage_count, _, length, feature_width = block_qkv.shape
    head_dim = feature_width // HEADS
    split_qkv = block_qkv.reshape(passage_count, 3, length, HEADS, head_dim).astype(jnp.float32)
    scores = jnp.einsum('pthd,puhd->phtu', split_qkv[:, 0], split_qkv[:, 1]) * head_dim ** (-0.5)
    row_max = lax.optimization_barrier(jnp.max(scores, axis=-1, keepdims=True))
    scaled = jnp.exp(scores - row_max)
    row_total = lax.optimization_barrier(jnp.sum(scaled, axis=-1, keepdims=True))
    self_lse = (row_max + jnp.log(row_total))[..., 0]
    self_probs = (scaled / row_total).astype(jnp.bfloat16)
    self_out = jnp.einsum('phtu,puhd->pthd', self_probs.astype(jnp.float32), split_qkv[:, 2])
    return (self_out.reshape(passage_count, length, feature_width).astype(jnp.bfloat16), self_lse)

def score_block(pass_q, pass_o, pass_lse, pass_resid, key_val, weights):
    w_o, ln_gain, ln_bias, w_dense, b_dense, w_out = weights
    passage_count, length, feature_width = pass_q.shape
    head_dim = feature_width // HEADS
    query_len = key_val.shape[1]
    token_rows = pass_q.reshape(passage_count * length, HEADS, head_dim).astype(jnp.float32)
    key_rows = key_val[0].reshape(query_len, HEADS, head_dim).astype(jnp.float32)
    value_rows = key_val[1].reshape(query_len, HEADS, head_dim).astype(jnp.float32)
    scores = jnp.einsum('rhd,ahd->har', token_rows, key_rows) * head_dim ** (-0.5)
    row_max = lax.optimization_barrier(jnp.max(scores, axis=1, keepdims=True))
    scaled = jnp.exp(scores - row_max)
    row_total = lax.optimization_barrier(jnp.sum(scaled, axis=1, keepdims=True))
    cross_lse = row_max[:, 0, :] + jnp.log(row_total[:, 0, :])
    self_lse = jnp.transpose(pass_lse, (1, 0, 2)).reshape(HEADS, passage_count * length)
    self_share = jax.nn.sigmoid(self_lse - cross_lse)
    spread = (1.0 - self_share)[:, None, :] * scaled / row_total
    key_weight = (lax.optimization_barrier(jnp.sum(spread.reshape(HEADS, query_len, passage_count, length), axis=3)) / length).astype(jnp.bfloat16)
    query_part = jnp.einsum('hab,ahd->bhd', key_weight.astype(jnp.float32), value_rows).reshape(passage_count, feature_width)
    token_weight = (self_share / length).astype(jnp.bfloat16).reshape(HEADS, passage_count, length)
    self_rows = pass_o.reshape(passage_count, length, HEADS, head_dim).astype(jnp.float32)
    self_part = jnp.einsum('hbt,bthd->bhd', token_weight.astype(jnp.float32), self_rows).reshape(passage_count, feature_width)
    pooled = (query_part + self_part).astype(jnp.bfloat16)
    mixed_rows = jnp.dot(pooled, w_o, preferred_element_type=jnp.float32) + pass_resid.astype(jnp.float32)
    row_mean = lax.optimization_barrier(jnp.mean(mixed_rows, axis=-1, keepdims=True))
    centered = mixed_rows - row_mean
    row_var = lax.optimization_barrier(jnp.mean(centered * centered, axis=-1, keepdims=True))
    normed = (centered * lax.rsqrt(row_var + norm_eps) * ln_gain + ln_bias).astype(jnp.bfloat16)
    hidden = jnp.tanh(jnp.dot(normed, w_dense, preferred_element_type=jnp.float32) + b_dense)
    return lax.optimization_barrier(jnp.sum(hidden * w_out, axis=-1))

def log_probs(scores, is_valid):
    masked = jnp.where(is_valid, scores, jnp.float32(-1e+30))
    row_max = lax.optimization_barrier(jnp.max(masked, axis=-1, keepdims=True))
    scaled = jnp.where(is_valid, jnp.exp(masked - row_max), jnp.float32(0.0))
    return scores - row_max - jnp.log(lax.optimization_barrier(jnp.sum(scaled, axis=-1, keepdims=True)))

def distill(teacher, student, is_valid):
    log_t = log_probs(teacher, is_valid)
    log_s = log_probs(student, is_valid)
    prob_t = jnp.where(is_valid, jnp.exp(log_t), jnp.float32(0.0))
    prob_s = jnp.where(is_valid, jnp.exp(log_s), jnp.float32(0.0))
    loss = lax.optimization_barrier(jnp.sum(jnp.where(is_valid, prob_t * (log_t - log_s), jnp.float32(0.0)), axis=-1))
    return (loss, prob_s - prob_t)

def reference(query_kv, student_query, block_holder, cand_local, counts, passage_qkv, passage_resid, student_passage, w_o, ln_gain, ln_bias, w_dense, b_dense, w_out):
    weights = (w_o, ln_gain, ln_bias, w_dense, b_dense, w_out)
    passage_total = passage_qkv.shape[0]
    groups = passage_qkv.reshape(passage_total // P_DEV, P_DEV, 3, P_LEN, D)
    self_outs, self_lses = lax.map(self_attend, groups)
    all_out = self_outs.reshape(passage_total, P_LEN, D)
    all_lse = self_lses.reshape(passage_total, HEADS, P_LEN)
    all_q = passage_qkv[:, 0]
    passage_ids = (block_holder[:, :, 0][:, :, None] * POOL + cand_local).astype(jnp.int32)

    def per_query(slot_item):
        key_val, query_embed, id_rows = slot_item

        def per_block(id_row):
            teacher = score_block(all_q[id_row], all_out[id_row], all_lse[id_row], passage_resid[id_row], key_val, weights)
            student = student_scale * jnp.dot(student_passage[id_row], query_embed, preferred_element_type=jnp.float32)
            return (teacher, student)
        teacher, student = lax.map(per_block, id_rows)
        return (teacher.reshape(-1), student.reshape(-1))
    teacher_raw, student_raw = lax.map(per_query, (query_kv, student_query, passage_ids))
    slot_count = CAND_BLOCKS * BLOCK
    is_valid = jnp.arange(slot_count, dtype=jnp.int32)[None, :] < counts[:, None]
    query_loss, score_grad = distill(teacher_raw, student_raw, is_valid)
    teacher_scores = jnp.where(is_valid, teacher_raw, jnp.float32(0.0))
    flat_ids = passage_ids.reshape(passage_ids.shape[0], slot_count)
    cand_embed = student_passage[flat_ids].astype(jnp.float32)
    grad_query = student_scale * jnp.einsum('qc,qcd->qd', score_grad, cand_embed, precision=lax.Precision.HIGHEST)
    terms = (score_grad[:, :, None] * student_query[:, None, :].astype(jnp.float32)).reshape(-1, D)
    grad_passage = student_scale * jax.ops.segment_sum(terms, flat_ids.reshape(-1), num_segments=passage_total)
    return (teacher_scores, query_loss, grad_query, grad_passage)
```

```python
import functools

import jax
import jax.numpy as jnp
from jax import lax
from jax.experimental import pallas as pl
from jax.experimental.pallas import tpu as pltpu
from jax.sharding import PartitionSpec as P

HEADS = 16
HEAD_DIM = 64
PAIRS = HEADS // 2
LANES = 128
student_scale = 0.125
norm_eps = 1e-05
VMEM_LIMIT = 56 * 1024 * 1024
NT = (((1,), (1,)), ((), ()))


def iota(shape, axis):
    return lax.broadcasted_iota(jnp.int32, shape, axis)


def pair_masks(rows):
    low = iota((rows, LANES), 1) < HEAD_DIM
    return low, jnp.logical_not(low)


def self_kernel(qkv_ref, out_ref, lse_ref):
    passages, _, length, _ = qkv_ref.shape
    rows = passages * length
    masks = pair_masks(rows)
    same = iota((rows, rows), 0) // length == iota((rows, rows), 1) // length

    def body(k, carry):
        lanes = pl.ds(pl.multiple_of(k * LANES, LANES), LANES)
        q = qkv_ref[:, 0, :, lanes].reshape(rows, LANES)
        key = qkv_ref[:, 1, :, lanes].reshape(rows, LANES)
        value = qkv_ref[:, 2, :, lanes].reshape(rows, LANES)
        outs, lses = [], []
        for mask in masks:
            q_head = jnp.where(mask, q.astype(jnp.float32) * 0.125, 0.0).astype(jnp.bfloat16)
            scores = lax.dot_general(key, q_head, NT, preferred_element_type=jnp.float32)
            scores = jnp.where(same, scores, -1e30)
            top = jnp.max(scores, axis=0, keepdims=True)
            scaled = jnp.exp(scores - top)
            total = jnp.sum(scaled, axis=0, keepdims=True)
            lses.append(top + jnp.log(total))
            probs = (scaled / total).T.astype(jnp.bfloat16)
            outs.append(jnp.dot(probs, value, preferred_element_type=jnp.float32))
        out_ref[:, lanes] = jnp.where(masks[0], outs[0], outs[1]).astype(jnp.bfloat16)
        lse_ref[k] = jnp.concatenate(lses, axis=0)
        return carry

    lax.fori_loop(0, PAIRS, body, 0)


def cross_kernel(k_ref, q_ref, so_ref, lse_ref, kwt_ref, part_ref):
    queries, keys, _ = k_ref.shape
    passages, _, length, _ = q_ref.shape
    rows = passages * length
    masks = pair_masks(rows)
    out_low = iota((queries * passages, LANES), 1) < HEAD_DIM
    own = (iota((passages, rows), 1) // length == iota((passages, rows), 0)).astype(jnp.float32)
    spots = [
        jnp.where(iota((rows, LANES), 1) == iota((rows, LANES), 0) // length + h * passages, 1.0 / length, 0.0).astype(
            jnp.bfloat16
        )
        for h in range(2)
    ]

    def body(k, carry):
        lanes = pl.ds(pl.multiple_of(k * LANES, LANES), LANES)
        q = q_ref[:, 0, :, lanes].reshape(rows, LANES)
        key = k_ref[:, :, lanes].reshape(queries * keys, LANES)
        so = so_ref[:, lanes]
        lse = lse_ref[k]
        weights, parts = None, []
        for h in range(2):
            q_head = jnp.where(masks[h], q.astype(jnp.float32) * 0.125, 0.0).astype(jnp.bfloat16)
            scores = lax.dot_general(key, q_head, NT, preferred_element_type=jnp.float32)
            scores = scores.reshape(queries, keys, rows)
            self_lse = lse[h : h + 1]
            top = jnp.maximum(jnp.max(scores, axis=1), self_lse)
            scaled = jnp.exp(scores - top[:, None, :])
            self_term = jnp.exp(self_lse - top)
            inverse = 1.0 / (jnp.sum(scaled, axis=1) + self_term)
            spread = (scaled * inverse[:, None, :]).reshape(queries * keys, rows).astype(jnp.bfloat16)
            weight = jnp.dot(spread, spots[h], preferred_element_type=jnp.float32)
            weights = weight if weights is None else weights + weight
            token = self_term * inverse * (1.0 / length)
            token = (token[:, None, :] * own[None]).reshape(queries * passages, rows).astype(jnp.bfloat16)
            parts.append(jnp.dot(token, so, preferred_element_type=jnp.float32))
        part_ref[:, lanes] = jnp.where(out_low, parts[0], parts[1])
        kwt_ref[k] = weights.T[: 2 * passages].astype(jnp.bfloat16)
        return carry

    lax.fori_loop(0, PAIRS, body, 0)


def head_kernel(v_ref, kwt_ref, part_ref, resid_ref, wo_ref, gain_ref, bias_ref, wd_ref, bd_ref, out_w_ref, teacher_ref, pooled, table):
    step = pl.program_id(0)
    queries, keys, width = v_ref.shape
    passages = resid_ref.shape[0]
    group = 8
    cols = group * keys
    span = 2 * passages
    own = (iota((group, span, cols), 2) // keys == iota((group, span, cols), 0)).astype(jnp.float32)
    low = iota((group, passages, LANES), 2) < HEAD_DIM

    def body(k, carry):
        lanes = pl.ds(pl.multiple_of(k * LANES, LANES), LANES)
        for c in range(queries // group):
            weight = kwt_ref[k, :, c * cols : (c + 1) * cols].astype(jnp.float32)
            weight = (weight[None] * own).reshape(group * span, cols).astype(jnp.bfloat16)
            value = v_ref[c * group : (c + 1) * group, :, lanes].reshape(cols, LANES)
            got = jnp.dot(weight, value, preferred_element_type=jnp.float32)
            got = got.reshape(group, 2, passages, LANES)
            got = jnp.where(low, got[:, 0], got[:, 1]).reshape(group * passages, LANES)
            rows = slice(c * group * passages, (c + 1) * group * passages)
            pooled[rows, lanes] = (got + part_ref[rows, lanes]).astype(jnp.bfloat16)
        return carry

    lax.fori_loop(0, PAIRS, body, 0)
    mixed = jnp.dot(pooled[...], wo_ref[...], preferred_element_type=jnp.float32)
    mixed = (mixed.reshape(queries, passages, width) + resid_ref[...].astype(jnp.float32)[None]).reshape(
        queries * passages, width
    )
    mean = jnp.mean(mixed, axis=-1, keepdims=True)
    centered = mixed - mean
    var = jnp.mean(centered * centered, axis=-1, keepdims=True)
    normed = (centered * lax.rsqrt(var + norm_eps) * gain_ref[...] + bias_ref[...]).astype(jnp.bfloat16)
    hidden = jnp.tanh(jnp.dot(normed, wd_ref[...], preferred_element_type=jnp.float32) + bd_ref[...])
    score = jnp.sum((hidden * out_w_ref[...]).reshape(queries, passages, width), axis=-1)
    table[pl.ds(pl.multiple_of(step * queries, queries), queries), :] = score

    @pl.when(step == pl.num_programs(0) - 1)
    def _():
        teacher_ref[...] = table[...].T


def split_dot(a, b):
    high = a.astype(jnp.bfloat16)
    low = (a - high.astype(jnp.float32)).astype(jnp.bfloat16)
    return jnp.dot(high, b, preferred_element_type=jnp.float32) + jnp.dot(low, b, preferred_element_type=jnp.float32)


def loss_kernel(teacher_ref, student_ref, count_ref, slot_ref, sp_ref, sq_ref, index_ref, score_ref, loss_ref, gq_ref, gp_ref, held, rows_held):
    teacher, student, count = teacher_ref[...], student_ref[...], count_ref[...]
    total, queries = teacher.shape
    slots = slot_ref.shape[1]
    passages = gp_ref.shape[0]
    index = index_ref[0]
    live = count > 0.0

    def log_probs(scores):
        top = jnp.max(jnp.where(live, scores, -1e30), axis=0, keepdims=True)
        scaled = jnp.where(live, count * jnp.exp(jnp.where(live, scores - top, 0.0)), 0.0)
        return scores - top - jnp.log(jnp.sum(scaled, axis=0, keepdims=True))

    log_t, log_s = log_probs(teacher), log_probs(student)
    prob_t = jnp.where(live, count * jnp.exp(jnp.where(live, log_t, 0.0)), 0.0)
    prob_s = jnp.where(live, count * jnp.exp(jnp.where(live, log_s, 0.0)), 0.0)
    loss = jnp.sum(jnp.where(live, prob_t * (log_t - log_s), 0.0), axis=0, keepdims=True)
    mine = iota((1, queries), 1) == index
    loss_ref[...] = jnp.sum(jnp.where(mine, loss, 0.0), axis=1, keepdims=True)
    own_teacher = jnp.sum(jnp.where(mine, teacher, 0.0), axis=1, keepdims=True)
    hit = iota((total, slots), 0) == slot_ref[...]
    score_ref[...] = jnp.sum(jnp.where(hit, own_teacher, 0.0), axis=0, keepdims=True)
    grad = (prob_s - prob_t) * student_scale
    held[...] = grad
    own = held[pl.ds(pl.multiple_of(index * passages, passages), passages), :]
    gp_ref[...] = split_dot(own, sq_ref[...])
    rows_held[...] = grad.T
    row = rows_held[pl.ds(index, 1), :]
    gq_ref[...] = split_dot(jnp.broadcast_to(row, (8, total)), sp_ref[...])[:1]


def call(kernel, **kw):
    return pl.pallas_call(kernel, compiler_params=pltpu.CompilerParams(vmem_limit_bytes=VMEM_LIMIT), **kw)


def local(n_pb, n_pa, query_kv, student_query, block_holder, cand_local, counts, passage_qkv, passage_resid, student_passage, w_o, ln_gain, ln_bias, w_dense, b_dense, w_out):
    f32, bf16 = jnp.float32, jnp.bfloat16
    axes = ("pb", "pa")
    column = lax.axis_index("pa")
    index = lax.axis_index("pb") * n_pa + column
    nq = n_pb * n_pa
    passages, _, length, width = passage_qkv.shape
    keys = query_kv.shape[2]
    rows = passages * length
    total = nq * passages
    blocks, slot_len = cand_local.shape[1:]
    slots = blocks * slot_len

    own_cand = lax.dynamic_slice_in_dim(cand_local, column, 1, 0)[0].astype(jnp.int32)
    own_holder = lax.dynamic_slice_in_dim(block_holder, column, 1, 0)[0]
    own_count = lax.dynamic_slice_in_dim(counts, column, 1, 0)
    own_id = ((own_cand // passages) * n_pa + own_holder) * passages + own_cand % passages
    own_id = own_id.reshape(1, slots)
    own_id = jnp.where(jnp.arange(slots, dtype=jnp.int32)[None, :] < own_count[:, None], own_id, -1)

    numbers = jnp.concatenate([own_cand.reshape(-1), own_holder.reshape(-1), own_count]).astype(bf16)
    numbers = jnp.pad(numbers, (0, width - numbers.shape[0]))[None]
    extra = jnp.concatenate([student_passage, student_query, numbers, jnp.zeros((16 - passages - 2, width), bf16)], axis=0)
    first = jnp.concatenate([query_kv[:, 0], extra[None]], axis=1)
    got = lax.all_gather(first, axes, axis=0, tiled=True)
    value = lax.all_gather(query_kv[:, 1], axes, axis=0, tiled=True)

    self_out, self_lse = call(
        self_kernel,
        out_shape=(jax.ShapeDtypeStruct((rows, width), bf16), jax.ShapeDtypeStruct((PAIRS, 2, rows), f32)),
    )(passage_qkv)

    chunk = 8
    kwt, part = call(
        cross_kernel,
        grid=(nq // chunk,),
        in_specs=[
            pl.BlockSpec((chunk, keys, width), lambda i: (i, 0, 0)),
            pl.BlockSpec((passages, 1, length, width), lambda i: (0, 0, 0, 0)),
            pl.BlockSpec((rows, width), lambda i: (0, 0)),
            pl.BlockSpec((PAIRS, 2, rows), lambda i: (0, 0, 0)),
        ],
        out_specs=(
            pl.BlockSpec((PAIRS, 2 * passages, chunk * keys), lambda i: (0, 0, i)),
            pl.BlockSpec((chunk * passages, width), lambda i: (i, 0)),
        ),
        out_shape=(
            jax.ShapeDtypeStruct((PAIRS, 2 * passages, nq * keys), bf16),
            jax.ShapeDtypeStruct((total, width), f32),
        ),
    )(got, passage_qkv, self_out, self_lse)

    sp = got[:, keys : keys + passages].reshape(total, width)
    sq = got[:, keys + passages]
    ints = got[:, keys + passages + 1, : slots + blocks + 1].astype(jnp.int32)
    cand = ints[:, :slots]
    holder = jnp.repeat(ints[:, slots : slots + blocks], slot_len, axis=1)
    ids = ((cand // passages) * n_pa + holder) * passages + cand % passages
    ids = jnp.where(jnp.arange(slots, dtype=jnp.int32)[None, :] < ints[:, slots + blocks :], ids, -1)
    count = jnp.sum((ids[None, :, :] == jnp.arange(total, dtype=jnp.int32)[:, None, None]).astype(f32), axis=2)
    student = student_scale * lax.dot_general(sp, sq, NT, preferred_element_type=f32)

    step = 16
    whole = lambda *shape: pl.BlockSpec(shape, lambda i: (0,) * len(shape))
    teacher = call(
        head_kernel,
        grid=(nq // step,),
        in_specs=[
            pl.BlockSpec((step, keys, width), lambda i: (i, 0, 0)),
            pl.BlockSpec((PAIRS, 2 * passages, step * keys), lambda i: (0, 0, i)),
            pl.BlockSpec((step * passages, width), lambda i: (i, 0)),
            whole(passages, width),
            whole(width, width),
            whole(1, width),
            whole(1, width),
            whole(width, width),
            whole(1, width),
            whole(1, width),
        ],
        out_specs=whole(passages, nq),
        out_shape=jax.ShapeDtypeStruct((passages, nq), f32),
        scratch_shapes=[pltpu.VMEM((step * passages, width), bf16), pltpu.VMEM((nq, passages), f32)],
    )(value, kwt, part, passage_resid, w_o, ln_gain[None], ln_bias[None], w_dense, b_dense[None], w_out[None])

    teacher_all = lax.all_gather(teacher, axes, axis=0, tiled=True)
    vmem = pl.BlockSpec(memory_space=pltpu.VMEM)
    scores, loss, grad_query, grad_passage = call(
        loss_kernel,
        in_specs=[vmem] * 6 + [pl.BlockSpec(memory_space=pltpu.SMEM)],
        out_shape=(
            jax.ShapeDtypeStruct((1, slots), f32),
            jax.ShapeDtypeStruct((1, 1), f32),
            jax.ShapeDtypeStruct((1, width), f32),
            jax.ShapeDtypeStruct((passages, width), f32),
        ),
        scratch_shapes=[pltpu.VMEM((total, nq), f32), pltpu.VMEM((nq, total), f32)],
    )(teacher_all, student, count, own_id, sp, sq, index.reshape(1).astype(jnp.int32))
    return scores, loss.reshape(1), grad_query, grad_passage


def solution(mesh):
    placed = (
        P(("pb", "pa"), None, None, None),
        P(("pb", "pa"), None),
        P("pb", None, None),
        P("pb", None, None),
        P("pb"),
        P(("pa", "pb"), None, None, None),
        P(("pa", "pb"), None),
        P(("pa", "pb"), None),
        P(),
        P(),
        P(),
        P(),
        P(),
        P(),
    )
    return jax.shard_map(
        functools.partial(local, mesh.shape["pb"], mesh.shape["pa"]),
        mesh=mesh,
        in_specs=placed,
        out_specs=(P(("pb", "pa"), None), P(("pb", "pa")), P(("pb", "pa"), None), P(("pa", "pb"), None)),
        check_vma=False,
    )
```

```python
import functools

import jax
import jax.numpy as jnp
from jax import lax
from jax.experimental import pallas as pl
from jax.experimental.pallas import tpu as pltpu
from jax.sharding import PartitionSpec as P

HEADS = 16
HEAD_DIM = 64
PAIRS = HEADS // 2
BLOCK = 32
BLOCKS = 2
LANES = 128
student_scale = 0.125
norm_eps = 1e-05
VMEM_LIMIT = 56 * 1024 * 1024
NT = (((1,), (1,)), ((), ()))


def iota(shape, axis):
    return lax.broadcasted_iota(jnp.int32, shape, axis)


def pair_masks(rows):
    low = iota((rows, LANES), 1) < HEAD_DIM
    return low, jnp.logical_not(low)


def attend_pair(qkv_ref, out_ref, lse_ref, k):
    passages, _, length, _ = qkv_ref.shape
    rows = passages * length
    masks = pair_masks(rows)
    same = iota((rows, rows), 0) // length == iota((rows, rows), 1) // length
    lanes = pl.ds(pl.multiple_of(k * LANES, LANES), LANES)
    q = qkv_ref[:, 0, :, lanes].reshape(rows, LANES)
    key = qkv_ref[:, 1, :, lanes].reshape(rows, LANES)
    value = qkv_ref[:, 2, :, lanes].reshape(rows, LANES)
    outs, lses = [], []
    for mask in masks:
        q_head = jnp.where(mask, q.astype(jnp.float32) * 0.125, 0.0).astype(jnp.bfloat16)
        scores = lax.dot_general(key, q_head, NT, preferred_element_type=jnp.float32)
        scores = jnp.where(same, scores, -1e30)
        top = jnp.max(scores, axis=0, keepdims=True)
        scaled = jnp.exp(scores - top)
        total = jnp.sum(scaled, axis=0, keepdims=True)
        lses.append(top + jnp.log(total))
        probs = (scaled * (1.0 / total)).T.astype(jnp.bfloat16)
        outs.append(jnp.dot(probs, value, preferred_element_type=jnp.float32))
    out_ref[:, lanes] = jnp.where(masks[0], outs[0], outs[1]).astype(jnp.bfloat16)
    lse_ref[k] = jnp.concatenate(lses, axis=0)


def gather_kernel(n_pb, n_pa, first_ref, value_ref, qkv_ref, got_ref, vals_ref, out_ref, lse_ref, send, recv, here):
    me_b, me_a = lax.axis_index("pb"), lax.axis_index("pa")
    core = me_b % 2
    spot = me_b // 2
    sx, sy = spot % 2, spot // 2
    beside = (sy * 2 + 1 - sx) * 2 + core
    across = ((1 - sy) * 2 + sx) * 2 + core
    corner = ((1 - sy) * 2 + 1 - sx) * 2 + core
    other = spot * 2 + 1 - core
    bufs = (got_ref, vals_ref)

    def copy(kind, piece, slot, owner_b, to_b, to_a):
        owner_a = (me_a + n_pa - slot) % n_pa
        ref = bufs[piece].at[owner_b * n_pa + owner_a]
        return pltpu.make_async_remote_copy(
            src_ref=ref,
            dst_ref=ref,
            send_sem=send.at[kind * 2 + piece, slot],
            recv_sem=recv.at[kind * 2 + piece, slot],
            device_id=(to_b, to_a),
            device_id_type=pl.DeviceIdType.MESH,
        )

    def along(piece, step):
        ref = bufs[piece].at[me_b * n_pa + me_a]
        return pltpu.make_async_remote_copy(
            src_ref=ref,
            dst_ref=ref,
            send_sem=send.at[piece, step],
            recv_sem=recv.at[piece, step],
            device_id=(me_b, (me_a + step) % n_pa),
            device_id_type=pl.DeviceIdType.MESH,
        )

    def arrived(kind, piece, slot, owner_b):
        copy(kind, piece, slot, owner_b, other, me_a).wait_recv()

    barrier = pltpu.get_barrier_semaphore()
    for peer in (beside, across, other):
        pl.semaphore_signal(barrier, inc=1, device_id=(peer, me_a), device_id_type=pl.DeviceIdType.MESH)

    def greet(step, carry):
        pl.semaphore_signal(
            barrier, inc=1, device_id=(me_b, (me_a + step) % n_pa), device_id_type=pl.DeviceIdType.MESH
        )
        return carry

    lax.fori_loop(1, n_pa, greet, 0)
    mine = me_b * n_pa + me_a
    own_copies = [
        pltpu.make_async_copy(first_ref.at[0], got_ref.at[mine], here.at[0]),
        pltpu.make_async_copy(value_ref.at[0], vals_ref.at[mine], here.at[1]),
    ]
    for one in own_copies:
        one.start()
    for one in own_copies:
        one.wait()
    pl.semaphore_wait(barrier, n_pa + 2)

    def column(step, carry):
        along(0, step).start()
        along(1, step).start()
        return carry

    def plane(slot, carry):
        @pl.when(slot > 0)
        def _():
            arrived(0, 0, slot, me_b)
            arrived(0, 1, slot, me_b)

        for piece in range(2):
            copy(1, piece, slot, me_b, beside, me_a).start()
            copy(2, piece, slot, me_b, across, me_a).start()
            copy(4, piece, slot, me_b, other, me_a).start()

        @pl.when(slot < 4)
        def _():
            for half in range(PAIRS // 4):
                attend_pair(qkv_ref, out_ref, lse_ref, slot * (PAIRS // 4) + half)

        return carry

    def forward(slot, carry):
        arrived(1, 0, slot, beside)
        copy(3, 0, slot, beside, across, me_a).start()
        copy(5, 0, slot, beside, other, me_a).start()
        arrived(2, 1, slot, across)
        copy(3, 1, slot, across, beside, me_a).start()
        copy(6, 1, slot, across, other, me_a).start()
        arrived(1, 1, slot, beside)
        copy(5, 1, slot, beside, other, me_a).start()
        arrived(2, 0, slot, across)
        copy(6, 0, slot, across, other, me_a).start()
        return carry

    def last(slot, carry):
        for piece in range(2):
            arrived(3, piece, slot, corner)
            copy(7, piece, slot, corner, other, me_a).start()
        return carry

    def finish(slot, carry):
        for piece in range(2):
            for kind, owner in ((4, me_b), (5, beside), (6, across), (7, corner)):
                far = owner + 1 - 2 * core
                arrived(kind, piece, slot, far)
                copy(kind, piece, slot, owner, other, me_a).wait_send()
            copy(1, piece, slot, me_b, beside, me_a).wait_send()
            copy(2, piece, slot, me_b, across, me_a).wait_send()
        copy(3, 0, slot, beside, across, me_a).wait_send()
        copy(3, 1, slot, across, beside, me_a).wait_send()

        @pl.when(slot > 0)
        def _():
            along(0, slot).wait_send()
            along(1, slot).wait_send()

        return carry

    lax.fori_loop(1, n_pa, column, 0)
    lax.fori_loop(0, n_pa, plane, 0)
    lax.fori_loop(0, n_pa, forward, 0)
    lax.fori_loop(0, n_pa, last, 0)
    lax.fori_loop(0, n_pa, finish, 0)


def share_kernel(n_pb, n_pa, own_ref, all_ref, send, recv, here):
    me_b, me_a = lax.axis_index("pb"), lax.axis_index("pa")
    count = n_pb * n_pa
    me = me_b * n_pa + me_a

    def place(step):
        to = (me + step) % count
        return (to // n_pa, to % n_pa)

    def copy(step):
        return pltpu.make_async_remote_copy(
            src_ref=own_ref,
            dst_ref=all_ref.at[me],
            send_sem=send.at[step],
            recv_sem=recv.at[step],
            device_id=place(step),
            device_id_type=pl.DeviceIdType.MESH,
        )

    def came(step):
        source = (me + count - step) % count
        return pltpu.make_async_remote_copy(
            src_ref=own_ref,
            dst_ref=all_ref.at[source],
            send_sem=send.at[step],
            recv_sem=recv.at[step],
            device_id=place(step),
            device_id_type=pl.DeviceIdType.MESH,
        )

    barrier = pltpu.get_barrier_semaphore()

    def greet(step, carry):
        pl.semaphore_signal(barrier, inc=1, device_id=place(step), device_id_type=pl.DeviceIdType.MESH)
        return carry

    def start(step, carry):
        copy(step).start()
        return carry

    def finish(step, carry):
        came(step).wait_recv()
        copy(step).wait_send()
        return carry

    lax.fori_loop(1, count, greet, 0)
    own_copy = pltpu.make_async_copy(own_ref, all_ref.at[me], here.at[0])
    own_copy.start()
    pl.semaphore_wait(barrier, count - 1)
    lax.fori_loop(1, count, start, 0)
    own_copy.wait()
    lax.fori_loop(1, count, finish, 0)


def list_kernel(n_pa, index_ref, extra_ref, sp_ref, sq_ref, student_ref, count_ref, order_ref, held):
    queries, _, width = extra_ref.shape
    total = sp_ref.shape[0]
    passages = total // queries
    extra = extra_ref[...].astype(jnp.float32)
    sp = extra[:, :passages].reshape(total, width).astype(jnp.bfloat16)
    rest = extra[:, passages:]
    sq = rest[:, 0].astype(jnp.bfloat16)
    sp_ref[...] = sp
    sq_ref[...] = sq
    student_ref[...] = student_scale * lax.dot_general(sp, sq, NT, preferred_element_type=jnp.float32)
    ids = rest[:, 1, :LANES].T
    slots = BLOCK * BLOCKS
    row = iota((total, queries), 0).astype(jnp.float32)
    number = jnp.floor(row / passages)
    part = row - number * passages
    group = jnp.floor(number / n_pa)
    holder_of = number - group * n_pa
    local_of = group * passages + part
    real = ids[slots + BLOCKS : slots + BLOCKS + 1]
    count = jnp.zeros((total, queries), jnp.float32)
    for b in range(BLOCKS):
        tally = jnp.zeros((total, queries), jnp.float32)
        for c in range(b * BLOCK, (b + 1) * BLOCK):
            name = jnp.where(real > c, ids[c : c + 1], -1.0)
            tally = tally + (local_of == name).astype(jnp.float32)
        count = count + jnp.where(holder_of == ids[slots + b : slots + b + 1], tally, 0.0)
    count_ref[...] = count
    held[...] = count
    own = held[pl.ds(pl.multiple_of(index_ref[0] * passages, passages), passages), :]
    need = (jnp.max(own, axis=0, keepdims=True) > 0.0).astype(jnp.float32)
    lane, col = iota((queries, queries), 0), iota((queries, queries), 1)
    need_col = jnp.sum(jnp.where(lane == col, need, 0.0), axis=1, keepdims=True)
    before = jnp.sum(jnp.where(lane < col, need_col, 0.0), axis=0, keepdims=True)
    needed = jnp.sum(need, axis=1, keepdims=True)
    spot = iota((1, queries), 1).astype(jnp.float32)
    place = jnp.where(need > 0.0, before, needed + spot - before)
    order = jnp.sum(jnp.where(place == lane.astype(jnp.float32), col.astype(jnp.float32), 0.0), axis=1, keepdims=True)
    order = jnp.sum(jnp.where(lane == col, order, 0.0), axis=0, keepdims=True)
    order_ref[...] = jnp.concatenate([order, jnp.broadcast_to(needed, (1, queries))], axis=0).astype(jnp.int32)


def cross_kernel(queries, order_ref, k_ref, q_ref, so_ref, lse_ref, kwt_ref, part_ref):
    step = pl.program_id(0)
    keys = k_ref.shape[1]
    passages, _, length, _ = q_ref.shape
    rows = passages * length
    masks = pair_masks(rows)
    out_low = iota((queries * passages, LANES), 1) < HEAD_DIM
    own = (iota((passages, rows), 1) // length == iota((passages, rows), 0)).astype(jnp.float32)
    spots = [
        jnp.where(iota((rows, LANES), 1) == iota((rows, LANES), 0) // length + h * passages, 1.0 / length, 0.0).astype(
            jnp.bfloat16
        )
        for h in range(2)
    ]

    def body(k, carry):
        lanes = pl.ds(pl.multiple_of(k * LANES, LANES), LANES)
        q = q_ref[:, 0, :, lanes].reshape(rows, LANES)
        key = jnp.concatenate([k_ref[order_ref[0, step * queries + i], :, lanes] for i in range(queries)], axis=0)
        so = so_ref[:, lanes]
        lse = lse_ref[k]
        weights, parts = None, []
        for h in range(2):
            q_head = jnp.where(masks[h], q.astype(jnp.float32) * 0.125, 0.0).astype(jnp.bfloat16)
            scores = lax.dot_general(key, q_head, NT, preferred_element_type=jnp.float32)
            scores = scores.reshape(queries, keys, rows)
            self_lse = lse[h : h + 1]
            top = jnp.maximum(jnp.max(scores, axis=1), self_lse)
            scaled = jnp.exp(scores - top[:, None, :])
            self_term = jnp.exp(self_lse - top)
            inverse = 1.0 / (jnp.sum(scaled, axis=1) + self_term)
            spread = (scaled * inverse[:, None, :]).reshape(queries * keys, rows).astype(jnp.bfloat16)
            weight = jnp.dot(spread, spots[h], preferred_element_type=jnp.float32)
            weights = weight if weights is None else weights + weight
            token = self_term * inverse * (1.0 / length)
            token = (token[:, None, :] * own[None]).reshape(queries * passages, rows).astype(jnp.bfloat16)
            parts.append(jnp.dot(token, so, preferred_element_type=jnp.float32))
        part_ref[:, lanes] = jnp.where(out_low, parts[0], parts[1])
        kwt_ref[k] = weights.T[: 2 * passages].astype(jnp.bfloat16)
        return carry

    @pl.when(step * queries < order_ref[1, 0])
    def _():
        lax.fori_loop(0, PAIRS, body, 0)


def head_kernel(queries, order_ref, v_ref, kwt_ref, part_ref, resid_ref, wo_ref, gain_ref, bias_ref, wd_ref, bd_ref, out_w_ref, teacher_ref, pooled, table):
    step = pl.program_id(0)
    _, keys, width = v_ref.shape
    passages = resid_ref.shape[0]
    group = 8
    cols = group * keys
    span = 2 * passages
    own = (iota((group, span, cols), 2) // keys == iota((group, span, cols), 0)).astype(jnp.float32)
    low = iota((group, passages, LANES), 2) < HEAD_DIM

    def body(k, carry):
        lanes = pl.ds(pl.multiple_of(k * LANES, LANES), LANES)
        for c in range(queries // group):
            weight = kwt_ref[k, :, c * cols : (c + 1) * cols].astype(jnp.float32)
            weight = (weight[None] * own).reshape(group * span, cols).astype(jnp.bfloat16)
            value = jnp.concatenate(
                [v_ref[order_ref[0, step * queries + c * group + i], :, lanes] for i in range(group)], axis=0
            )
            got = jnp.dot(weight, value, preferred_element_type=jnp.float32)
            got = got.reshape(group, 2, passages, LANES)
            got = jnp.where(low, got[:, 0], got[:, 1]).reshape(group * passages, LANES)
            rows = slice(c * group * passages, (c + 1) * group * passages)
            pooled[rows, lanes] = (got + part_ref[rows, lanes]).astype(jnp.bfloat16)
        return carry

    @pl.when(step == 0)
    def _():
        table[...] = jnp.zeros_like(table)

    @pl.when(step * queries < order_ref[1, 0])
    def _():
        lax.fori_loop(0, PAIRS, body, 0)
        mixed = jnp.dot(pooled[...], wo_ref[...], preferred_element_type=jnp.float32)
        mixed = (mixed.reshape(queries, passages, width) + resid_ref[...].astype(jnp.float32)[None]).reshape(
            queries * passages, width
        )
        mean = jnp.mean(mixed, axis=-1, keepdims=True)
        centered = mixed - mean
        var = jnp.mean(centered * centered, axis=-1, keepdims=True)
        normed = (centered * lax.rsqrt(var + norm_eps) * gain_ref[...] + bias_ref[...]).astype(jnp.bfloat16)
        hidden = jnp.tanh(jnp.dot(normed, wd_ref[...], preferred_element_type=jnp.float32) + bd_ref[...])
        score = jnp.sum((hidden * out_w_ref[...]).reshape(queries, passages, width), axis=-1)
        for i in range(queries):
            table[pl.ds(order_ref[0, step * queries + i], 1), :] = score[i : i + 1]

    @pl.when(step == pl.num_programs(0) - 1)
    def _():
        teacher_ref[...] = table[...].T


def split_dot(a, b):
    high = a.astype(jnp.bfloat16)
    low = (a - high.astype(jnp.float32)).astype(jnp.bfloat16)
    return jnp.dot(high, b, preferred_element_type=jnp.float32) + jnp.dot(low, b, preferred_element_type=jnp.float32)


def loss_kernel(teacher_ref, student_ref, count_ref, slot_ref, sp_ref, sq_ref, index_ref, score_ref, loss_ref, gq_ref, gp_ref, held, rows_held):
    teacher, student, count = teacher_ref[...], student_ref[...], count_ref[...]
    total, queries = teacher.shape
    slots = slot_ref.shape[1]
    passages = gp_ref.shape[0]
    index = index_ref[0]
    live = count > 0.0

    def log_probs(scores):
        top = jnp.max(jnp.where(live, scores, -1e30), axis=0, keepdims=True)
        scaled = jnp.where(live, count * jnp.exp(jnp.where(live, scores - top, 0.0)), 0.0)
        return scores - top - jnp.log(jnp.sum(scaled, axis=0, keepdims=True))

    log_t, log_s = log_probs(teacher), log_probs(student)
    prob_t = jnp.where(live, count * jnp.exp(jnp.where(live, log_t, 0.0)), 0.0)
    prob_s = jnp.where(live, count * jnp.exp(jnp.where(live, log_s, 0.0)), 0.0)
    loss = jnp.sum(jnp.where(live, prob_t * (log_t - log_s), 0.0), axis=0, keepdims=True)
    mine = iota((1, queries), 1) == index
    loss_ref[...] = jnp.sum(jnp.where(mine, loss, 0.0), axis=1, keepdims=True)
    own_teacher = jnp.sum(jnp.where(mine, teacher, 0.0), axis=1, keepdims=True)
    hit = iota((total, slots), 0) == slot_ref[...]
    score_ref[...] = jnp.sum(jnp.where(hit, own_teacher, 0.0), axis=0, keepdims=True)
    grad = (prob_s - prob_t) * student_scale
    held[...] = grad
    own = held[pl.ds(pl.multiple_of(index * passages, passages), passages), :]
    gp_ref[...] = split_dot(own, sq_ref[...])
    rows_held[...] = grad.T
    row = rows_held[pl.ds(index, 1), :]
    gq_ref[...] = split_dot(jnp.broadcast_to(row, (8, total)), sp_ref[...])[:1]


def call(kernel, **kw):
    return pl.pallas_call(kernel, compiler_params=pltpu.CompilerParams(vmem_limit_bytes=VMEM_LIMIT), **kw)


def remote_call(kernel, number, **kw):
    params = pltpu.CompilerParams(vmem_limit_bytes=VMEM_LIMIT, collective_id=number, has_side_effects=True)
    return pl.pallas_call(kernel, compiler_params=params, **kw)


def local(n_pb, n_pa, query_kv, student_query, block_holder, cand_local, counts, passage_qkv, passage_resid, student_passage, w_o, ln_gain, ln_bias, w_dense, b_dense, w_out):
    f32, bf16 = jnp.float32, jnp.bfloat16
    axes = ("pb", "pa")
    column = lax.axis_index("pa")
    index = lax.axis_index("pb") * n_pa + column
    nq = n_pb * n_pa
    passages, _, length, width = passage_qkv.shape
    keys = query_kv.shape[2]
    rows = passages * length
    total = nq * passages
    blocks, slot_len = cand_local.shape[1:]
    slots = blocks * slot_len

    own_cand = lax.dynamic_slice_in_dim(cand_local, column, 1, 0)[0].astype(jnp.int32)
    own_holder = lax.dynamic_slice_in_dim(block_holder, column, 1, 0)[0]
    own_count = lax.dynamic_slice_in_dim(counts, column, 1, 0)
    own_id = ((own_cand // passages) * n_pa + own_holder) * passages + own_cand % passages
    own_id = own_id.reshape(1, slots)
    own_id = jnp.where(jnp.arange(slots, dtype=jnp.int32)[None, :] < own_count[:, None], own_id, -1)

    numbers = jnp.concatenate([own_cand.reshape(-1), own_holder.reshape(-1), own_count]).astype(bf16)
    numbers = jnp.pad(numbers, (0, width - numbers.shape[0]))[None]
    extra = jnp.concatenate([student_passage, student_query, numbers, jnp.zeros((16 - passages - 2, width), bf16)], axis=0)
    first = jnp.concatenate([query_kv[:, 0], extra[None]], axis=1)
    anywhere, vmem, smem = (pl.BlockSpec(memory_space=m) for m in (pl.ANY, pltpu.VMEM, pltpu.SMEM))
    got, value, self_out, self_lse = remote_call(
        functools.partial(gather_kernel, n_pb, n_pa),
        1,
        in_specs=[anywhere, anywhere, vmem],
        out_specs=(anywhere, anywhere, vmem, vmem),
        out_shape=(
            jax.ShapeDtypeStruct((nq,) + first.shape[1:], bf16),
            jax.ShapeDtypeStruct((nq, keys, width), bf16),
            jax.ShapeDtypeStruct((rows, width), bf16),
            jax.ShapeDtypeStruct((PAIRS, 2, rows), f32),
        ),
        scratch_shapes=[
            pltpu.SemaphoreType.DMA((16, n_pa)),
            pltpu.SemaphoreType.DMA((16, n_pa)),
            pltpu.SemaphoreType.DMA((2,)),
        ],
    )(first, query_kv[:, 1], passage_qkv)

    device = index.reshape(1).astype(jnp.int32)
    sp, sq, student, count, order = call(
        functools.partial(list_kernel, n_pa),
        grid=(1,),
        in_specs=[smem, pl.BlockSpec((nq, 16, width), lambda i: (0, keys // 16, 0))],
        out_specs=tuple(
            pl.BlockSpec(shape, lambda i: (0, 0)) for shape in ((total, width), (nq, width), (total, nq), (total, nq), (2, nq))
        ),
        out_shape=(
            jax.ShapeDtypeStruct((total, width), bf16),
            jax.ShapeDtypeStruct((nq, width), bf16),
            jax.ShapeDtypeStruct((total, nq), f32),
            jax.ShapeDtypeStruct((total, nq), f32),
            jax.ShapeDtypeStruct((2, nq), jnp.int32),
        ),
        scratch_shapes=[pltpu.VMEM((total, nq), f32)],
    )(device, got)

    whole = lambda *shape: pl.BlockSpec(shape, lambda i, o: (0,) * len(shape))
    chunk = 8
    kwt, part = call(
        functools.partial(cross_kernel, chunk),
        grid_spec=pltpu.PrefetchScalarGridSpec(
            num_scalar_prefetch=1,
            grid=(nq // chunk,),
            in_specs=[
                whole(nq, keys, width),
                whole(passages, 1, length, width),
                whole(rows, width),
                whole(PAIRS, 2, rows),
            ],
            out_specs=(
                pl.BlockSpec((PAIRS, 2 * passages, chunk * keys), lambda i, o: (0, 0, i)),
                pl.BlockSpec((chunk * passages, width), lambda i, o: (i, 0)),
            ),
        ),
        out_shape=(
            jax.ShapeDtypeStruct((PAIRS, 2 * passages, nq * keys), bf16),
            jax.ShapeDtypeStruct((total, width), f32),
        ),
    )(order, got, passage_qkv, self_out, self_lse)

    step = 16
    teacher = call(
        functools.partial(head_kernel, step),
        grid_spec=pltpu.PrefetchScalarGridSpec(
            num_scalar_prefetch=1,
            grid=(nq // step,),
            in_specs=[
                whole(nq, keys, width),
                pl.BlockSpec((PAIRS, 2 * passages, step * keys), lambda i, o: (0, 0, i)),
                pl.BlockSpec((step * passages, width), lambda i, o: (i, 0)),
                whole(passages, width),
                whole(width, width),
                whole(1, width),
                whole(1, width),
                whole(width, width),
                whole(1, width),
                whole(1, width),
            ],
            out_specs=whole(passages, nq),
            scratch_shapes=[pltpu.VMEM((step * passages, width), bf16), pltpu.VMEM((nq, passages), f32)],
        ),
        out_shape=jax.ShapeDtypeStruct((passages, nq), f32),
    )(order, value, kwt, part, passage_resid, w_o, ln_gain[None], ln_bias[None], w_dense, b_dense[None], w_out[None])

    teacher_all = remote_call(
        functools.partial(share_kernel, n_pb, n_pa),
        2,
        in_specs=[vmem],
        out_specs=vmem,
        out_shape=jax.ShapeDtypeStruct((nq, passages, nq), f32),
        scratch_shapes=[
            pltpu.SemaphoreType.DMA((nq,)),
            pltpu.SemaphoreType.DMA((nq,)),
            pltpu.SemaphoreType.DMA((1,)),
        ],
    )(teacher).reshape(total, nq)
    scores, loss, grad_query, grad_passage = call(
        loss_kernel,
        in_specs=[vmem] * 6 + [smem],
        out_shape=(
            jax.ShapeDtypeStruct((1, slots), f32),
            jax.ShapeDtypeStruct((1, 1), f32),
            jax.ShapeDtypeStruct((1, width), f32),
            jax.ShapeDtypeStruct((passages, width), f32),
        ),
        scratch_shapes=[pltpu.VMEM((total, nq), f32), pltpu.VMEM((nq, total), f32)],
    )(teacher_all, student, count, own_id, sp, sq, device)
    return scores, loss.reshape(1), grad_query, grad_passage


def solution(mesh):
    placed = (
        P(("pb", "pa"), None, None, None),
        P(("pb", "pa"), None),
        P("pb", None, None),
        P("pb", None, None),
        P("pb"),
        P(("pa", "pb"), None, None, None),
        P(("pa", "pb"), None),
        P(("pa", "pb"), None),
        P(),
        P(),
        P(),
        P(),
        P(),
        P(),
    )
    return jax.shard_map(
        functools.partial(local, mesh.shape["pb"], mesh.shape["pa"]),
        mesh=mesh,
        in_specs=placed,
        out_specs=(P(("pb", "pa"), None), P(("pb", "pa")), P(("pb", "pa"), None), P(("pa", "pb"), None)),
        check_vma=False,
    )
```

```python
import functools

import jax
import jax.numpy as jnp
from jax import lax
from jax.experimental import pallas as pl
from jax.experimental.pallas import tpu as pltpu
from jax.sharding import PartitionSpec as P

HEADS = 16
HEAD_DIM = 64
PAIRS = HEADS // 2
BLOCK = 32
BLOCKS = 2
LANES = 128
student_scale = 0.125
norm_eps = 1e-05
VMEM_LIMIT = 56 * 1024 * 1024
NT = (((1,), (1,)), ((), ()))


def iota(shape, axis):
    return lax.broadcasted_iota(jnp.int32, shape, axis)


def pair_masks(rows):
    low = iota((rows, LANES), 1) < HEAD_DIM
    return low, jnp.logical_not(low)


def attend_pair(qkv_ref, out_ref, lse_ref, k):
    passages, _, length, _ = qkv_ref.shape
    rows = passages * length
    masks = pair_masks(rows)
    same = iota((rows, rows), 0) // length == iota((rows, rows), 1) // length
    lanes = pl.ds(pl.multiple_of(k * LANES, LANES), LANES)
    q = qkv_ref[:, 0, :, lanes].reshape(rows, LANES)
    key = qkv_ref[:, 1, :, lanes].reshape(rows, LANES)
    value = qkv_ref[:, 2, :, lanes].reshape(rows, LANES)
    outs, lses = [], []
    for mask in masks:
        q_head = jnp.where(mask, q.astype(jnp.float32) * 0.125, 0.0).astype(jnp.bfloat16)
        scores = lax.dot_general(key, q_head, NT, preferred_element_type=jnp.float32)
        scores = jnp.where(same, scores, -1e30)
        top = jnp.max(scores, axis=0, keepdims=True)
        scaled = jnp.exp(scores - top)
        total = jnp.sum(scaled, axis=0, keepdims=True)
        lses.append(top + jnp.log(total))
        probs = (scaled * (1.0 / total)).T.astype(jnp.bfloat16)
        outs.append(jnp.dot(probs, value, preferred_element_type=jnp.float32))
    out_ref[:, lanes] = jnp.where(masks[0], outs[0], outs[1]).astype(jnp.bfloat16)
    lse_ref[k] = jnp.concatenate(lses, axis=0)


def gather_kernel(
    n_pb, n_pa, kv_ref, qkv_ref, sp_ref, sq_ref, cand_ref, holder_ref, count_ref,
    got_ref, vals_ref, more_ref, out_ref, lse_ref, wide, packed, send, recv, here,
):
    me_b, me_a = lax.axis_index("pb"), lax.axis_index("pa")
    core = me_b % 2
    spot = me_b // 2
    sx, sy = spot % 2, spot // 2
    beside = (sy * 2 + 1 - sx) * 2 + core
    across = ((1 - sy) * 2 + sx) * 2 + core
    corner = ((1 - sy) * 2 + 1 - sx) * 2 + core
    other = spot * 2 + 1 - core
    bufs = (got_ref, vals_ref, more_ref)
    pieces = range(3)
    mesh_ids = pl.DeviceIdType.MESH

    def copy(kind, piece, owner_a, owner_b, to_b, to_a, landing=None):
        ref = bufs[piece].at[owner_b * n_pa + owner_a]
        landing = kind if landing is None else landing
        return pltpu.make_async_remote_copy(
            src_ref=ref,
            dst_ref=ref,
            send_sem=send.at[kind * 3 + piece, owner_a],
            recv_sem=recv.at[landing * 3 + piece, owner_a],
            device_id=(to_b, to_a),
            device_id_type=mesh_ids,
        )

    def up(piece, owner_a):
        return copy(0, piece, owner_a, me_b, me_b, me_a + 1)

    def down(piece, owner_a):
        return copy(8, piece, owner_a, me_b, me_b, me_a - 1, landing=0)

    def arrived(kind, piece, owner_a, owner_b):
        copy(kind, piece, owner_a, owner_b, other, me_a).wait_recv()

    barrier = pltpu.get_barrier_semaphore()
    for peer in (beside, across, other):
        pl.semaphore_signal(barrier, inc=1, device_id=(peer, me_a), device_id_type=mesh_ids)

    @pl.when(me_a + 1 < n_pa)
    def _():
        pl.semaphore_signal(barrier, inc=1, device_id=(me_b, me_a + 1), device_id_type=mesh_ids)

    @pl.when(me_a > 0)
    def _():
        pl.semaphore_signal(barrier, inc=1, device_id=(me_b, me_a - 1), device_id_type=mesh_ids)

    passages = sp_ref.shape[0]
    width = sp_ref.shape[1]
    mine = me_b * n_pa + me_a
    own_copies = [
        pltpu.make_async_copy(kv_ref.at[0, 0], got_ref.at[mine], here.at[0]),
        pltpu.make_async_copy(kv_ref.at[0, 1], vals_ref.at[mine], here.at[1]),
        pltpu.make_async_copy(packed, more_ref.at[mine], here.at[2]),
    ]
    own_copies[0].start()
    own_copies[1].start()
    wide[...] = jnp.zeros_like(wide)
    wide[:passages] = sp_ref[...].astype(jnp.float32)
    wide[passages : passages + 1] = sq_ref[...].astype(jnp.float32)
    wide[passages + 1 : passages + 2] = jnp.full((1, width), count_ref[me_a].astype(jnp.float32))
    wide[passages + 2 : passages + 2 + BLOCKS, :BLOCK] = cand_ref[me_a].astype(jnp.float32)
    wide[passages + 2 + BLOCKS : passages + 2 + 2 * BLOCKS] = jnp.broadcast_to(
        holder_ref[me_a].astype(jnp.float32), (BLOCKS, width)
    )
    packed[...] = wide[...].astype(jnp.bfloat16)
    own_copies[2].start()
    for one in own_copies:
        one.wait()

    @pl.when((me_a > 0) & (me_a + 1 < n_pa))
    def _():
        pl.semaphore_wait(barrier, 5)

    @pl.when((me_a == 0) | (me_a + 1 == n_pa))
    def _():
        pl.semaphore_wait(barrier, 4)

    def column(owner, fresh):
        if not fresh:
            for piece in pieces:
                arrived(0, piece, owner, me_b)

        @pl.when((owner <= me_a) & (me_a + 1 < n_pa))
        def _():
            for piece in pieces:
                up(piece, owner).start()

        @pl.when((owner >= me_a) & (me_a > 0))
        def _():
            for piece in pieces:
                down(piece, owner).start()

        for piece in pieces:
            copy(1, piece, owner, me_b, beside, me_a).start()
            copy(2, piece, owner, me_b, across, me_a).start()
        for piece in pieces:
            copy(4, piece, owner, me_b, other, me_a).start()

    def forward(owner):
        for piece in pieces:
            near, kind = (across, 2) if piece == 1 else (beside, 1)
            arrived(kind, piece, owner, near)
            copy(3, piece, owner, near, beside if piece == 1 else across, me_a).start()
            copy(6 if piece == 1 else 5, piece, owner, near, other, me_a).start()
        for piece in pieces:
            near, kind = (beside, 1) if piece == 1 else (across, 2)
            arrived(kind, piece, owner, near)
            copy(5 if piece == 1 else 6, piece, owner, near, other, me_a).start()

    def last(owner):
        for piece in pieces:
            arrived(3, piece, owner, corner)
            copy(7, piece, owner, corner, other, me_a).start()

    def both(distance, act):
        for owner in (me_a - distance, me_a + distance):
            @pl.when((owner >= 0) & (owner < n_pa))
            def _(owner=owner):
                act(owner)

    def stage(distance, carry):
        @pl.when(distance < n_pa)
        def _():
            both(distance, lambda owner: column(owner, False))

        @pl.when(distance < 4)
        def _():
            for half in range(PAIRS // 4):
                attend_pair(qkv_ref, out_ref, lse_ref, distance * (PAIRS // 4) + half)

        @pl.when(distance == 1)
        def _():
            forward(me_a)

        @pl.when((distance > 1) & (distance <= n_pa))
        def _():
            both(distance - 1, forward)

        @pl.when(distance == 2)
        def _():
            last(me_a)

        @pl.when(distance > 2)
        def _():
            both(distance - 2, last)

        return carry

    def finish(owner, carry):
        for piece in pieces:
            for kind, near in ((4, me_b), (5, beside), (6, across), (7, corner)):
                arrived(kind, piece, owner, near + 1 - 2 * core)
                copy(kind, piece, owner, near, other, me_a).wait_send()
            copy(1, piece, owner, me_b, beside, me_a).wait_send()
            copy(2, piece, owner, me_b, across, me_a).wait_send()
            if piece == 1:
                copy(3, piece, owner, across, beside, me_a).wait_send()
            else:
                copy(3, piece, owner, beside, across, me_a).wait_send()

        @pl.when((owner <= me_a) & (me_a + 1 < n_pa))
        def _():
            for piece in pieces:
                up(piece, owner).wait_send()

        @pl.when((owner >= me_a) & (me_a > 0))
        def _():
            for piece in pieces:
                down(piece, owner).wait_send()

        return carry

    column(me_a, True)
    for half in range(PAIRS // 4):
        attend_pair(qkv_ref, out_ref, lse_ref, half)
    lax.fori_loop(1, n_pa + 2, stage, 0)
    lax.fori_loop(0, n_pa, finish, 0)


def share_kernel(n_pb, n_pa, own_ref, all_ref, send, recv, here):
    me_b, me_a = lax.axis_index("pb"), lax.axis_index("pa")
    count = n_pb * n_pa
    me = me_b * n_pa + me_a

    def place(step):
        to = (me + step) % count
        return (to // n_pa, to % n_pa)

    def copy(step):
        return pltpu.make_async_remote_copy(
            src_ref=own_ref,
            dst_ref=all_ref.at[me],
            send_sem=send.at[step],
            recv_sem=recv.at[step],
            device_id=place(step),
            device_id_type=pl.DeviceIdType.MESH,
        )

    def came(step):
        source = (me + count - step) % count
        return pltpu.make_async_remote_copy(
            src_ref=own_ref,
            dst_ref=all_ref.at[source],
            send_sem=send.at[step],
            recv_sem=recv.at[step],
            device_id=place(step),
            device_id_type=pl.DeviceIdType.MESH,
        )

    barrier = pltpu.get_barrier_semaphore()

    def greet(step, carry):
        pl.semaphore_signal(barrier, inc=1, device_id=place(step), device_id_type=pl.DeviceIdType.MESH)
        return carry

    def start(step, carry):
        copy(step).start()
        return carry

    def finish(step, carry):
        came(step).wait_recv()
        copy(step).wait_send()
        return carry

    lax.fori_loop(1, count, greet, 0)
    own_copy = pltpu.make_async_copy(own_ref, all_ref.at[me], here.at[0])
    own_copy.start()
    pl.semaphore_wait(barrier, count - 1)
    lax.fori_loop(1, count, start, 0)
    own_copy.wait()
    lax.fori_loop(1, count, finish, 0)


def list_kernel(n_pa, index_ref, extra_ref, sp_ref, sq_ref, student_ref, count_ref, order_ref, slot_ref, held):
    queries, _, width = extra_ref.shape
    total = sp_ref.shape[0]
    passages = total // queries
    extra = extra_ref[...].astype(jnp.float32)
    sp = extra[:, :passages].reshape(total, width).astype(jnp.bfloat16)
    rest = extra[:, passages:]
    sq = rest[:, 0].astype(jnp.bfloat16)
    sp_ref[...] = sp
    sq_ref[...] = sq
    student_ref[...] = student_scale * lax.dot_general(sp, sq, NT, preferred_element_type=jnp.float32)
    real = rest[:, 1, :LANES].T[:1]
    ids = [rest[:, 2 + b, :LANES].T for b in range(BLOCKS)]
    holders = [rest[:, 2 + BLOCKS + b, :LANES].T[:1] for b in range(BLOCKS)]
    own_rest = extra_ref[pl.ds(index_ref[0], 1)].astype(jnp.float32)[0, passages:]
    slot = own_rest[2 : 2 + BLOCKS, :BLOCK]
    slot_group = jnp.floor(slot / passages)
    slot_id = (slot_group * n_pa + own_rest[2 + BLOCKS : 2 + 2 * BLOCKS, :BLOCK]) * passages + slot - slot_group * passages
    number_of = (iota((BLOCKS, BLOCK), 0) * BLOCK + iota((BLOCKS, BLOCK), 1)).astype(jnp.float32)
    slot_ref[...] = jnp.where(number_of < own_rest[1:2, :BLOCK], slot_id, -1.0).astype(jnp.int32)
    row = iota((total, queries), 0).astype(jnp.float32)
    number = jnp.floor(row / passages)
    part = row - number * passages
    group = jnp.floor(number / n_pa)
    holder_of = number - group * n_pa
    local_of = group * passages + part
    count = jnp.zeros((total, queries), jnp.float32)
    for b in range(BLOCKS):
        tally = jnp.zeros((total, queries), jnp.float32)
        for c in range(BLOCK):
            name = jnp.where(real > b * BLOCK + c, ids[b][c : c + 1], -1.0)
            tally = tally + (local_of == name).astype(jnp.float32)
        count = count + jnp.where(holder_of == holders[b], tally, 0.0)
    count_ref[...] = count
    held[...] = count
    own = held[pl.ds(pl.multiple_of(index_ref[0] * passages, passages), passages), :]
    need = (jnp.max(own, axis=0, keepdims=True) > 0.0).astype(jnp.float32)
    lane, col = iota((queries, queries), 0), iota((queries, queries), 1)
    need_col = jnp.sum(jnp.where(lane == col, need, 0.0), axis=1, keepdims=True)
    before = jnp.sum(jnp.where(lane < col, need_col, 0.0), axis=0, keepdims=True)
    needed = jnp.sum(need, axis=1, keepdims=True)
    spot = iota((1, queries), 1).astype(jnp.float32)
    place = jnp.where(need > 0.0, before, needed + spot - before)
    order = jnp.sum(jnp.where(place == lane.astype(jnp.float32), col.astype(jnp.float32), 0.0), axis=1, keepdims=True)
    order = jnp.sum(jnp.where(lane == col, order, 0.0), axis=0, keepdims=True)
    order_ref[...] = jnp.concatenate([order, jnp.broadcast_to(needed, (1, queries))], axis=0).astype(jnp.int32)


def cross_kernel(queries, order_ref, k_ref, q_ref, so_ref, lse_ref, kwt_ref, part_ref):
    step = pl.program_id(0)
    keys = k_ref.shape[1]
    passages, _, length, _ = q_ref.shape
    rows = passages * length
    masks = pair_masks(rows)
    out_low = iota((queries * passages, LANES), 1) < HEAD_DIM
    own = (iota((passages, rows), 1) // length == iota((passages, rows), 0)).astype(jnp.float32)
    spots = [
        jnp.where(iota((rows, LANES), 1) == iota((rows, LANES), 0) // length + h * passages, 1.0 / length, 0.0).astype(
            jnp.bfloat16
        )
        for h in range(2)
    ]

    def body(k, carry):
        lanes = pl.ds(pl.multiple_of(k * LANES, LANES), LANES)
        q = q_ref[:, 0, :, lanes].reshape(rows, LANES)
        key = jnp.concatenate([k_ref[order_ref[0, step * queries + i], :, lanes] for i in range(queries)], axis=0)
        so = so_ref[:, lanes]
        lse = lse_ref[k]
        weights, parts = None, []
        for h in range(2):
            q_head = jnp.where(masks[h], q.astype(jnp.float32) * 0.125, 0.0).astype(jnp.bfloat16)
            scores = lax.dot_general(key, q_head, NT, preferred_element_type=jnp.float32)
            scores = scores.reshape(queries, keys, rows)
            self_lse = lse[h : h + 1]
            top = jnp.maximum(jnp.max(scores, axis=1), self_lse)
            scaled = jnp.exp(scores - top[:, None, :])
            self_term = jnp.exp(self_lse - top)
            inverse = 1.0 / (jnp.sum(scaled, axis=1) + self_term)
            spread = (scaled * inverse[:, None, :]).reshape(queries * keys, rows).astype(jnp.bfloat16)
            weight = jnp.dot(spread, spots[h], preferred_element_type=jnp.float32)
            weights = weight if weights is None else weights + weight
            token = self_term * inverse * (1.0 / length)
            token = (token[:, None, :] * own[None]).reshape(queries * passages, rows).astype(jnp.bfloat16)
            parts.append(jnp.dot(token, so, preferred_element_type=jnp.float32))
        part_ref[:, lanes] = jnp.where(out_low, parts[0], parts[1])
        kwt_ref[k] = weights.T[: 2 * passages].astype(jnp.bfloat16)
        return carry

    @pl.when(step * queries < order_ref[1, 0])
    def _():
        lax.fori_loop(0, PAIRS, body, 0, unroll=4)


def head_kernel(queries, order_ref, v_ref, kwt_ref, part_ref, resid_ref, wo_ref, gain_ref, bias_ref, wd_ref, bd_ref, out_w_ref, teacher_ref, pooled, table):
    step = pl.program_id(0)
    _, keys, width = v_ref.shape
    passages = resid_ref.shape[0]
    group = 8
    cols = group * keys
    span = 2 * passages
    own = (iota((group, span, cols), 2) // keys == iota((group, span, cols), 0)).astype(jnp.float32)
    low = iota((group, passages, LANES), 2) < HEAD_DIM

    def body(k, carry):
        lanes = pl.ds(pl.multiple_of(k * LANES, LANES), LANES)
        for c in range(queries // group):
            weight = kwt_ref[k, :, c * cols : (c + 1) * cols].astype(jnp.float32)
            weight = (weight[None] * own).reshape(group * span, cols).astype(jnp.bfloat16)
            value = jnp.concatenate(
                [v_ref[order_ref[0, step * queries + c * group + i], :, lanes] for i in range(group)], axis=0
            )
            got = jnp.dot(weight, value, preferred_element_type=jnp.float32)
            got = got.reshape(group, 2, passages, LANES)
            got = jnp.where(low, got[:, 0], got[:, 1]).reshape(group * passages, LANES)
            rows = slice(c * group * passages, (c + 1) * group * passages)
            pooled[rows, lanes] = (got + part_ref[rows, lanes]).astype(jnp.bfloat16)
        return carry

    @pl.when(step == 0)
    def _():
        table[...] = jnp.zeros_like(table)

    @pl.when(step * queries < order_ref[1, 0])
    def _():
        lax.fori_loop(0, PAIRS, body, 0, unroll=4)
        mixed = jnp.dot(pooled[...], wo_ref[...], preferred_element_type=jnp.float32)
        mixed = (mixed.reshape(queries, passages, width) + resid_ref[...].astype(jnp.float32)[None]).reshape(
            queries * passages, width
        )
        mean = jnp.mean(mixed, axis=-1, keepdims=True)
        centered = mixed - mean
        var = jnp.mean(centered * centered, axis=-1, keepdims=True)
        normed = (centered * lax.rsqrt(var + norm_eps) * gain_ref[...] + bias_ref[...]).astype(jnp.bfloat16)
        hidden = jnp.tanh(jnp.dot(normed, wd_ref[...], preferred_element_type=jnp.float32) + bd_ref[...])
        score = jnp.sum((hidden * out_w_ref[...]).reshape(queries, passages, width), axis=-1)
        for i in range(queries):
            table[pl.ds(order_ref[0, step * queries + i], 1), :] = score[i : i + 1]

    @pl.when(step == pl.num_programs(0) - 1)
    def _():
        teacher_ref[...] = table[...].T


def split_dot(a, b):
    high = a.astype(jnp.bfloat16)
    low = (a - high.astype(jnp.float32)).astype(jnp.bfloat16)
    return jnp.dot(high, b, preferred_element_type=jnp.float32) + jnp.dot(low, b, preferred_element_type=jnp.float32)


def loss_kernel(teacher_ref, student_ref, count_ref, slot_ref, sp_ref, sq_ref, index_ref, score_ref, loss_ref, gq_ref, gp_ref, held, rows_held):
    teacher, student, count = teacher_ref[...], student_ref[...], count_ref[...]
    total, queries = teacher.shape
    passages = gp_ref.shape[0]
    index = index_ref[0]
    live = count > 0.0

    def log_probs(scores):
        top = jnp.max(jnp.where(live, scores, -1e30), axis=0, keepdims=True)
        scaled = jnp.where(live, count * jnp.exp(jnp.where(live, scores - top, 0.0)), 0.0)
        return scores - top - jnp.log(jnp.sum(scaled, axis=0, keepdims=True))

    log_t, log_s = log_probs(teacher), log_probs(student)
    prob_t = jnp.where(live, count * jnp.exp(jnp.where(live, log_t, 0.0)), 0.0)
    prob_s = jnp.where(live, count * jnp.exp(jnp.where(live, log_s, 0.0)), 0.0)
    loss = jnp.sum(jnp.where(live, prob_t * (log_t - log_s), 0.0), axis=0, keepdims=True)
    mine = iota((1, queries), 1) == index
    loss_ref[...] = jnp.sum(jnp.where(mine, loss, 0.0), axis=1, keepdims=True)
    own_teacher = jnp.sum(jnp.where(mine, teacher, 0.0), axis=1, keepdims=True)
    for b in range(BLOCKS):
        hit = iota((total, BLOCK), 0) == slot_ref[b : b + 1]
        score_ref[:, b * BLOCK : (b + 1) * BLOCK] = jnp.sum(jnp.where(hit, own_teacher, 0.0), axis=0, keepdims=True)
    grad = (prob_s - prob_t) * student_scale
    held[...] = grad
    own = held[pl.ds(pl.multiple_of(index * passages, passages), passages), :]
    gp_ref[...] = split_dot(own, sq_ref[...])
    rows_held[...] = grad.T
    row = rows_held[pl.ds(index, 1), :]
    gq_ref[...] = split_dot(jnp.broadcast_to(row, (8, total)), sp_ref[...])[:1]


def call(kernel, **kw):
    return pl.pallas_call(kernel, compiler_params=pltpu.CompilerParams(vmem_limit_bytes=VMEM_LIMIT), **kw)


def remote_call(kernel, number, **kw):
    params = pltpu.CompilerParams(vmem_limit_bytes=VMEM_LIMIT, collective_id=number, has_side_effects=True)
    return pl.pallas_call(kernel, compiler_params=params, **kw)


def local(n_pb, n_pa, query_kv, student_query, block_holder, cand_local, counts, passage_qkv, passage_resid, student_passage, w_o, ln_gain, ln_bias, w_dense, b_dense, w_out):
    f32, bf16 = jnp.float32, jnp.bfloat16
    axes = ("pb", "pa")
    column = lax.axis_index("pa")
    index = lax.axis_index("pb") * n_pa + column
    nq = n_pb * n_pa
    passages, _, length, width = passage_qkv.shape
    keys = query_kv.shape[2]
    rows = passages * length
    total = nq * passages
    blocks, slot_len = cand_local.shape[1:]
    slots = blocks * slot_len

    anywhere, vmem, smem = (pl.BlockSpec(memory_space=m) for m in (pl.ANY, pltpu.VMEM, pltpu.SMEM))
    got, value, more, self_out, self_lse = remote_call(
        functools.partial(gather_kernel, n_pb, n_pa),
        1,
        in_specs=[anywhere, vmem, vmem, vmem, vmem, vmem, smem],
        out_specs=(anywhere, anywhere, anywhere, vmem, vmem),
        out_shape=(
            jax.ShapeDtypeStruct((nq, keys, width), bf16),
            jax.ShapeDtypeStruct((nq, keys, width), bf16),
            jax.ShapeDtypeStruct((nq, 16, width), bf16),
            jax.ShapeDtypeStruct((rows, width), bf16),
            jax.ShapeDtypeStruct((PAIRS, 2, rows), f32),
        ),
        scratch_shapes=[
            pltpu.VMEM((16, width), f32),
            pltpu.VMEM((16, width), bf16),
            pltpu.SemaphoreType.DMA((27, n_pa)),
            pltpu.SemaphoreType.DMA((24, n_pa)),
            pltpu.SemaphoreType.DMA((3,)),
        ],
    )(query_kv, passage_qkv, student_passage, student_query, cand_local, block_holder, counts)

    device = index.reshape(1).astype(jnp.int32)
    sp, sq, student, count, order, own_id = call(
        functools.partial(list_kernel, n_pa),
        in_specs=[smem, vmem],
        out_shape=(
            jax.ShapeDtypeStruct((total, width), bf16),
            jax.ShapeDtypeStruct((nq, width), bf16),
            jax.ShapeDtypeStruct((total, nq), f32),
            jax.ShapeDtypeStruct((total, nq), f32),
            jax.ShapeDtypeStruct((2, nq), jnp.int32),
            jax.ShapeDtypeStruct((blocks, slot_len), jnp.int32),
        ),
        scratch_shapes=[pltpu.VMEM((total, nq), f32)],
    )(device, more)

    whole = lambda *shape: pl.BlockSpec(shape, lambda i, o: (0,) * len(shape))
    chunk = 8
    kwt, part = call(
        functools.partial(cross_kernel, chunk),
        grid_spec=pltpu.PrefetchScalarGridSpec(
            num_scalar_prefetch=1,
            grid=(nq // chunk,),
            in_specs=[
                whole(nq, keys, width),
                whole(passages, 1, length, width),
                whole(rows, width),
                whole(PAIRS, 2, rows),
            ],
            out_specs=(
                pl.BlockSpec((PAIRS, 2 * passages, chunk * keys), lambda i, o: (0, 0, i)),
                pl.BlockSpec((chunk * passages, width), lambda i, o: (i, 0)),
            ),
        ),
        out_shape=(
            jax.ShapeDtypeStruct((PAIRS, 2 * passages, nq * keys), bf16),
            jax.ShapeDtypeStruct((total, width), f32),
        ),
    )(order, got, passage_qkv, self_out, self_lse)

    step = 16
    teacher = call(
        functools.partial(head_kernel, step),
        grid_spec=pltpu.PrefetchScalarGridSpec(
            num_scalar_prefetch=1,
            grid=(nq // step,),
            in_specs=[
                whole(nq, keys, width),
                pl.BlockSpec((PAIRS, 2 * passages, step * keys), lambda i, o: (0, 0, i)),
                pl.BlockSpec((step * passages, width), lambda i, o: (i, 0)),
                whole(passages, width),
                whole(width, width),
                whole(1, width),
                whole(1, width),
                whole(width, width),
                whole(1, width),
                whole(1, width),
            ],
            out_specs=whole(passages, nq),
            scratch_shapes=[pltpu.VMEM((step * passages, width), bf16), pltpu.VMEM((nq, passages), f32)],
        ),
        out_shape=jax.ShapeDtypeStruct((passages, nq), f32),
    )(order, value, kwt, part, passage_resid, w_o, ln_gain[None], ln_bias[None], w_dense, b_dense[None], w_out[None])

    teacher_all = remote_call(
        functools.partial(share_kernel, n_pb, n_pa),
        2,
        in_specs=[vmem],
        out_specs=vmem,
        out_shape=jax.ShapeDtypeStruct((nq, passages, nq), f32),
        scratch_shapes=[
            pltpu.SemaphoreType.DMA((nq,)),
            pltpu.SemaphoreType.DMA((nq,)),
            pltpu.SemaphoreType.DMA((1,)),
        ],
    )(teacher).reshape(total, nq)
    scores, loss, grad_query, grad_passage = call(
        loss_kernel,
        in_specs=[vmem] * 6 + [smem],
        out_shape=(
            jax.ShapeDtypeStruct((1, slots), f32),
            jax.ShapeDtypeStruct((1, 1), f32),
            jax.ShapeDtypeStruct((1, width), f32),
            jax.ShapeDtypeStruct((passages, width), f32),
        ),
        scratch_shapes=[pltpu.VMEM((total, nq), f32), pltpu.VMEM((nq, total), f32)],
    )(teacher_all, student, count, own_id, sp, sq, device)
    return scores, loss.reshape(1), grad_query, grad_passage


def solution(mesh):
    placed = (
        P(("pb", "pa"), None, None, None),
        P(("pb", "pa"), None),
        P("pb", None, None),
        P("pb", None, None),
        P("pb"),
        P(("pa", "pb"), None, None, None),
        P(("pa", "pb"), None),
        P(("pa", "pb"), None),
        P(),
        P(),
        P(),
        P(),
        P(),
        P(),
    )
    return jax.shard_map(
        functools.partial(local, mesh.shape["pb"], mesh.shape["pa"]),
        mesh=mesh,
        in_specs=placed,
        out_specs=(P(("pb", "pa"), None), P(("pb", "pa")), P(("pb", "pa"), None), P(("pa", "pb"), None)),
        check_vma=False,
    )
```

```python
import functools

import jax
import jax.numpy as jnp
from jax import lax
from jax.experimental import pallas as pl
from jax.experimental.pallas import tpu as pltpu
from jax.sharding import PartitionSpec as P

HEADS = 16
HEAD_DIM = 64
PAIRS = HEADS // 2
BLOCK = 32
BLOCKS = 2
LANES = 128
student_scale = 0.125
norm_eps = 1e-05
VMEM_LIMIT = 56 * 1024 * 1024
NT = (((1,), (1,)), ((), ()))


def iota(shape, axis):
    return lax.broadcasted_iota(jnp.int32, shape, axis)


def pair_masks(rows):
    low = iota((rows, LANES), 1) < HEAD_DIM
    return low, jnp.logical_not(low)


def attend_pair(qkv_ref, out_ref, lse_ref, k):
    passages, _, length, _ = qkv_ref.shape
    rows = passages * length
    masks = pair_masks(rows)
    same = iota((rows, rows), 0) // length == iota((rows, rows), 1) // length
    lanes = pl.ds(pl.multiple_of(k * LANES, LANES), LANES)
    q = qkv_ref[:, 0, :, lanes].reshape(rows, LANES)
    key = qkv_ref[:, 1, :, lanes].reshape(rows, LANES)
    value = qkv_ref[:, 2, :, lanes].reshape(rows, LANES)
    outs, lses = [], []
    for mask in masks:
        q_head = jnp.where(mask, q.astype(jnp.float32) * 0.125, 0.0).astype(jnp.bfloat16)
        scores = lax.dot_general(key, q_head, NT, preferred_element_type=jnp.float32)
        scores = jnp.where(same, scores, -1e30)
        top = jnp.max(scores, axis=0, keepdims=True)
        scaled = jnp.exp(scores - top)
        total = jnp.sum(scaled, axis=0, keepdims=True)
        lses.append(top + jnp.log(total))
        probs = (scaled * (1.0 / total)).T.astype(jnp.bfloat16)
        outs.append(jnp.dot(probs, value, preferred_element_type=jnp.float32))
    out_ref[:, lanes] = jnp.where(masks[0], outs[0], outs[1]).astype(jnp.bfloat16)
    lse_ref[k] = jnp.concatenate(lses, axis=0)


def gather_kernel(
    n_pb, n_pa, kv_ref, qkv_ref, sp_ref, sq_ref, cand_ref, holder_ref, count_ref,
    vals_ref, more_ref, kwt_ref, part_ref, got_ref, out_ref, lse_ref, wide, packed, send, recv, here,
):
    me_b, me_a = lax.axis_index("pb"), lax.axis_index("pa")
    core = me_b % 2
    spot = me_b // 2
    sx, sy = spot % 2, spot // 2
    beside = (sy * 2 + 1 - sx) * 2 + core
    across = ((1 - sy) * 2 + sx) * 2 + core
    corner = ((1 - sy) * 2 + 1 - sx) * 2 + core
    other = spot * 2 + 1 - core
    bufs = (got_ref, vals_ref, more_ref)
    pieces = range(3)
    mesh_ids = pl.DeviceIdType.MESH

    def copy(kind, piece, owner_a, owner_b, to_b, to_a, landing=None):
        ref = bufs[piece].at[owner_b * n_pa + owner_a]
        landing = kind if landing is None else landing
        return pltpu.make_async_remote_copy(
            src_ref=ref,
            dst_ref=ref,
            send_sem=send.at[kind * 3 + piece, owner_a],
            recv_sem=recv.at[landing * 3 + piece, owner_a],
            device_id=(to_b, to_a),
            device_id_type=mesh_ids,
        )

    def up(piece, owner_a):
        return copy(0, piece, owner_a, me_b, me_b, me_a + 1)

    def down(piece, owner_a):
        return copy(8, piece, owner_a, me_b, me_b, me_a - 1, landing=0)

    def arrived(kind, piece, owner_a, owner_b):
        copy(kind, piece, owner_a, owner_b, other, me_a).wait_recv()

    barrier = pltpu.get_barrier_semaphore()
    for peer in (beside, across, other):
        pl.semaphore_signal(barrier, inc=1, device_id=(peer, me_a), device_id_type=mesh_ids)

    @pl.when(me_a + 1 < n_pa)
    def _():
        pl.semaphore_signal(barrier, inc=1, device_id=(me_b, me_a + 1), device_id_type=mesh_ids)

    @pl.when(me_a > 0)
    def _():
        pl.semaphore_signal(barrier, inc=1, device_id=(me_b, me_a - 1), device_id_type=mesh_ids)

    passages = sp_ref.shape[0]
    width = sp_ref.shape[1]
    mine = me_b * n_pa + me_a
    own_copies = [
        pltpu.make_async_copy(kv_ref.at[0, 0], got_ref.at[mine], here.at[0]),
        pltpu.make_async_copy(kv_ref.at[0, 1], vals_ref.at[mine], here.at[1]),
        pltpu.make_async_copy(packed, more_ref.at[mine], here.at[2]),
    ]
    own_copies[0].start()
    own_copies[1].start()
    wide[...] = jnp.zeros_like(wide)
    wide[:passages] = sp_ref[...].astype(jnp.float32)
    wide[passages : passages + 1] = sq_ref[...].astype(jnp.float32)
    wide[passages + 1 : passages + 2] = jnp.full((1, width), count_ref[me_a].astype(jnp.float32))
    wide[passages + 2 : passages + 2 + BLOCKS, :BLOCK] = cand_ref[me_a].astype(jnp.float32)
    wide[passages + 2 + BLOCKS : passages + 2 + 2 * BLOCKS] = jnp.broadcast_to(
        holder_ref[me_a].astype(jnp.float32), (BLOCKS, width)
    )
    packed[...] = wide[...].astype(jnp.bfloat16)
    own_copies[2].start()
    for one in own_copies:
        one.wait()

    @pl.when((me_a > 0) & (me_a + 1 < n_pa))
    def _():
        pl.semaphore_wait(barrier, 5)

    @pl.when((me_a == 0) | (me_a + 1 == n_pa))
    def _():
        pl.semaphore_wait(barrier, 4)

    def column(owner, fresh):
        if not fresh:
            for piece in pieces:
                arrived(0, piece, owner, me_b)

        @pl.when((owner <= me_a) & (me_a + 1 < n_pa))
        def _():
            for piece in pieces:
                up(piece, owner).start()

        @pl.when((owner >= me_a) & (me_a > 0))
        def _():
            for piece in pieces:
                down(piece, owner).start()

        for piece in pieces:
            copy(1, piece, owner, me_b, beside, me_a).start()
            copy(2, piece, owner, me_b, across, me_a).start()
        for piece in pieces:
            copy(4, piece, owner, me_b, other, me_a).start()

    def forward(owner):
        for piece in pieces:
            near, kind = (across, 2) if piece == 1 else (beside, 1)
            arrived(kind, piece, owner, near)
            copy(3, piece, owner, near, beside if piece == 1 else across, me_a).start()
            copy(6 if piece == 1 else 5, piece, owner, near, other, me_a).start()
        for piece in pieces:
            near, kind = (beside, 1) if piece == 1 else (across, 2)
            arrived(kind, piece, owner, near)
            copy(5 if piece == 1 else 6, piece, owner, near, other, me_a).start()

    def last(owner):
        for piece in pieces:
            arrived(3, piece, owner, corner)
            copy(7, piece, owner, corner, other, me_a).start()

    def both(distance, act):
        for owner in (me_a - distance, me_a + distance):
            @pl.when((owner >= 0) & (owner < n_pa))
            def _(owner=owner):
                act(owner)

    def stage(distance, carry):
        @pl.when(distance < n_pa)
        def _():
            both(distance, lambda owner: column(owner, False))

        @pl.when(distance == 1)
        def _():
            forward(me_a)

        @pl.when((distance > 1) & (distance <= n_pa))
        def _():
            both(distance - 1, forward)

        @pl.when(distance == 2)
        def _():
            last(me_a)

        @pl.when((distance > 2) & (distance <= n_pa + 1))
        def _():
            both(distance - 2, last)

        @pl.when(distance < 4)
        def _():
            for half in range(PAIRS // 4):
                attend_pair(qkv_ref, out_ref, lse_ref, distance * (PAIRS // 4) + half)

        def score(side, inner):
            owner = me_a + (2 * side - 1) * (distance - 3)

            @pl.when((owner >= 0) & (owner < n_pa) & ((distance > 3) | (side > 0)))
            def _():
                for kind, near in ((4, me_b), (5, beside), (6, across), (7, corner)):
                    arrived(kind, 0, owner, near + 1 - 2 * core)
                cross_group(got_ref, qkv_ref, out_ref, lse_ref, kwt_ref, part_ref, owner, n_pb, n_pa)

            return inner

        @pl.when(distance > 2)
        def _():
            lax.fori_loop(0, 2, score, 0)

        return carry

    def finish(owner, carry):
        for piece in pieces:
            for kind, near in ((4, me_b), (5, beside), (6, across), (7, corner)):
                if piece > 0:
                    arrived(kind, piece, owner, near + 1 - 2 * core)
                copy(kind, piece, owner, near, other, me_a).wait_send()
            copy(1, piece, owner, me_b, beside, me_a).wait_send()
            copy(2, piece, owner, me_b, across, me_a).wait_send()
            if piece == 1:
                copy(3, piece, owner, across, beside, me_a).wait_send()
            else:
                copy(3, piece, owner, beside, across, me_a).wait_send()

        @pl.when((owner <= me_a) & (me_a + 1 < n_pa))
        def _():
            for piece in pieces:
                up(piece, owner).wait_send()

        @pl.when((owner >= me_a) & (me_a > 0))
        def _():
            for piece in pieces:
                down(piece, owner).wait_send()

        return carry

    column(me_a, True)
    for half in range(PAIRS // 4):
        attend_pair(qkv_ref, out_ref, lse_ref, half)
    lax.fori_loop(1, n_pa + 3, stage, 0)
    lax.fori_loop(0, n_pa, finish, 0)


def share_kernel(n_pb, n_pa, own_ref, all_ref, send, recv, here):
    me_b, me_a = lax.axis_index("pb"), lax.axis_index("pa")
    mesh_ids = pl.DeviceIdType.MESH

    def column(step, from_a):
        return pltpu.make_async_remote_copy(
            src_ref=own_ref,
            dst_ref=all_ref.at[me_b, from_a],
            send_sem=send.at[step],
            recv_sem=recv.at[step],
            device_id=(me_b, (me_a + step) % n_pa),
            device_id_type=mesh_ids,
        )

    def plane(step, from_b):
        return pltpu.make_async_remote_copy(
            src_ref=all_ref.at[from_b],
            dst_ref=all_ref.at[from_b],
            send_sem=send.at[n_pa + step],
            recv_sem=recv.at[n_pa + step],
            device_id=((me_b + step) % n_pb, me_a),
            device_id_type=mesh_ids,
        )

    def loop(first, last, act):
        def one(step, carry):
            act(step)
            return carry

        lax.fori_loop(first, last, one, 0)

    barrier = pltpu.get_barrier_semaphore()

    def greet_column(step):
        pl.semaphore_signal(barrier, inc=1, device_id=(me_b, (me_a + step) % n_pa), device_id_type=mesh_ids)

    def greet_plane(step):
        pl.semaphore_signal(barrier, inc=1, device_id=((me_b + step) % n_pb, me_a), device_id_type=mesh_ids)

    loop(1, n_pa, greet_column)
    loop(1, n_pb, greet_plane)
    own_copy = pltpu.make_async_copy(own_ref, all_ref.at[me_b, me_a], here.at[0])
    own_copy.start()
    pl.semaphore_wait(barrier, n_pa + n_pb - 2)
    loop(1, n_pa, lambda step: column(step, me_a).start())
    own_copy.wait()
    loop(1, n_pa, lambda step: column(step, (me_a + n_pa - step) % n_pa).wait_recv())
    loop(1, n_pb, lambda step: plane(step, me_b).start())
    loop(1, n_pb, lambda step: plane(step, (me_b + n_pb - step) % n_pb).wait_recv())
    loop(1, n_pa, lambda step: column(step, me_a).wait_send())
    loop(1, n_pb, lambda step: plane(step, me_b).wait_send())


def list_kernel(n_pa, index_ref, extra_ref, sp_ref, sq_ref, student_ref, count_ref, slot_ref):
    queries, _, width = extra_ref.shape
    total = sp_ref.shape[0]
    passages = total // queries
    extra = extra_ref[...].astype(jnp.float32)
    sp = extra[:, :passages].reshape(total, width).astype(jnp.bfloat16)
    rest = extra[:, passages:]
    sq = rest[:, 0].astype(jnp.bfloat16)
    sp_ref[...] = sp
    sq_ref[...] = sq
    student_ref[...] = student_scale * lax.dot_general(sp, sq, NT, preferred_element_type=jnp.float32)
    real = rest[:, 1, :LANES].T[:1]
    ids = [rest[:, 2 + b, :LANES].T for b in range(BLOCKS)]
    holders = [rest[:, 2 + BLOCKS + b, :LANES].T[:1] for b in range(BLOCKS)]
    own_rest = extra_ref[pl.ds(index_ref[0], 1)].astype(jnp.float32)[0, passages:]
    slot = own_rest[2 : 2 + BLOCKS, :BLOCK]
    slot_group = jnp.floor(slot / passages)
    slot_id = (slot_group * n_pa + own_rest[2 + BLOCKS : 2 + 2 * BLOCKS, :BLOCK]) * passages + slot - slot_group * passages
    number_of = (iota((BLOCKS, BLOCK), 0) * BLOCK + iota((BLOCKS, BLOCK), 1)).astype(jnp.float32)
    slot_ref[...] = jnp.where(number_of < own_rest[1:2, :BLOCK], slot_id, -1.0).astype(jnp.int32)
    row = iota((total, queries), 0).astype(jnp.float32)
    number = jnp.floor(row / passages)
    part = row - number * passages
    group = jnp.floor(number / n_pa)
    holder_of = number - group * n_pa
    local_of = group * passages + part
    count = jnp.zeros((total, queries), jnp.float32)
    for b in range(BLOCKS):
        tally = jnp.zeros((total, queries), jnp.float32)
        for c in range(BLOCK):
            name = jnp.where(real > b * BLOCK + c, ids[b][c : c + 1], -1.0)
            tally = tally + (local_of == name).astype(jnp.float32)
        count = count + jnp.where(holder_of == holders[b], tally, 0.0)
    count_ref[...] = count


def cross_group(k_ref, q_ref, so_ref, lse_ref, kwt_ref, part_ref, owner, n_pb, n_pa):
    keys = k_ref.shape[1]
    passages, _, length, _ = q_ref.shape
    rows = passages * length
    masks = pair_masks(rows)
    out_low = iota((n_pb * passages, LANES), 1) < HEAD_DIM
    own = (iota((passages, rows), 1) // length == iota((passages, rows), 0)).astype(jnp.float32)
    spots = [
        jnp.where(iota((rows, LANES), 1) == iota((rows, LANES), 0) // length + h * passages, 1.0 / length, 0.0).astype(
            jnp.bfloat16
        )
        for h in range(2)
    ]

    def body(k, carry):
        lanes = pl.ds(pl.multiple_of(k * LANES, LANES), LANES)
        q = q_ref[:, 0, :, lanes].reshape(rows, LANES)
        key = jnp.concatenate([k_ref[i * n_pa + owner, :, lanes] for i in range(n_pb)], axis=0)
        so = so_ref[:, lanes]
        lse = lse_ref[k]
        weights, parts = None, []
        for h in range(2):
            q_head = jnp.where(masks[h], q.astype(jnp.float32) * 0.125, 0.0).astype(jnp.bfloat16)
            scores = lax.dot_general(key, q_head, NT, preferred_element_type=jnp.float32)
            scores = scores.reshape(n_pb, keys, rows)
            self_lse = lse[h : h + 1]
            top = jnp.maximum(jnp.max(scores, axis=1), self_lse)
            scaled = jnp.exp(scores - top[:, None, :])
            self_term = jnp.exp(self_lse - top)
            inverse = 1.0 / (jnp.sum(scaled, axis=1) + self_term)
            spread = (scaled * inverse[:, None, :]).reshape(n_pb * keys, rows).astype(jnp.bfloat16)
            weight = jnp.dot(spread, spots[h], preferred_element_type=jnp.float32)
            weights = weight if weights is None else weights + weight
            token = self_term * inverse * (1.0 / length)
            token = (token[:, None, :] * own[None]).reshape(n_pb * passages, rows).astype(jnp.bfloat16)
            parts.append(jnp.dot(token, so, preferred_element_type=jnp.float32))
        part_ref[owner, :, lanes] = jnp.where(out_low, parts[0], parts[1])
        kwt_ref[owner, k] = weights.T[: 2 * passages].astype(jnp.bfloat16)
        return carry

    lax.fori_loop(0, PAIRS, body, 0, unroll=4)


def head_kernel(queries, n_pa, v_ref, kwt_ref, part_ref, resid_ref, wo_ref, gain_ref, bias_ref, wd_ref, bd_ref, out_w_ref, teacher_ref, pooled, table):
    step = pl.program_id(0)
    _, keys, width = v_ref.shape
    passages = resid_ref.shape[0]
    groups, _, _, cols = kwt_ref.shape
    group = cols // keys
    span = 2 * passages
    own = (iota((group, span, cols), 2) // keys == iota((group, span, cols), 0)).astype(jnp.float32)
    low = iota((group, passages, LANES), 2) < HEAD_DIM

    def body(k, carry):
        lanes = pl.ds(pl.multiple_of(k * LANES, LANES), LANES)
        for c in range(groups):
            weight = kwt_ref[c, k].astype(jnp.float32)
            weight = (weight[None] * own).reshape(group * span, cols).astype(jnp.bfloat16)
            value = jnp.concatenate(
                [v_ref[i * n_pa + step * groups + c, :, lanes] for i in range(group)], axis=0
            )
            got = jnp.dot(weight, value, preferred_element_type=jnp.float32)
            got = got.reshape(group, 2, passages, LANES)
            got = jnp.where(low, got[:, 0], got[:, 1]).reshape(group * passages, LANES)
            rows = slice(c * group * passages, (c + 1) * group * passages)
            pooled[rows, lanes] = (got + part_ref[c, :, lanes]).astype(jnp.bfloat16)
        return carry

    @pl.when(step == 0)
    def _():
        table[...] = jnp.zeros_like(table)

    @pl.when(step >= 0)
    def _():
        lax.fori_loop(0, PAIRS, body, 0, unroll=4)
        mixed = jnp.dot(pooled[...], wo_ref[...], preferred_element_type=jnp.float32)
        mixed = (mixed.reshape(queries, passages, width) + resid_ref[...].astype(jnp.float32)[None]).reshape(
            queries * passages, width
        )
        mean = jnp.mean(mixed, axis=-1, keepdims=True)
        centered = mixed - mean
        var = jnp.mean(centered * centered, axis=-1, keepdims=True)
        normed = (centered * lax.rsqrt(var + norm_eps) * gain_ref[...] + bias_ref[...]).astype(jnp.bfloat16)
        hidden = jnp.tanh(jnp.dot(normed, wd_ref[...], preferred_element_type=jnp.float32) + bd_ref[...])
        score = jnp.sum((hidden * out_w_ref[...]).reshape(queries, passages, width), axis=-1)
        for i in range(queries):
            table[pl.ds(i % group * n_pa + step * groups + i // group, 1), :] = score[i : i + 1]

    @pl.when(step == pl.num_programs(0) - 1)
    def _():
        teacher_ref[...] = table[...].T


def split_dot(a, b):
    high = a.astype(jnp.bfloat16)
    low = (a - high.astype(jnp.float32)).astype(jnp.bfloat16)
    return jnp.dot(high, b, preferred_element_type=jnp.float32) + jnp.dot(low, b, preferred_element_type=jnp.float32)


def loss_kernel(teacher_ref, student_ref, count_ref, slot_ref, sp_ref, sq_ref, index_ref, score_ref, loss_ref, gq_ref, gp_ref, held, rows_held):
    teacher, student, count = teacher_ref[...], student_ref[...], count_ref[...]
    total, queries = teacher.shape
    passages = gp_ref.shape[0]
    index = index_ref[0]
    live = count > 0.0

    def log_probs(scores):
        top = jnp.max(jnp.where(live, scores, -1e30), axis=0, keepdims=True)
        scaled = jnp.where(live, count * jnp.exp(jnp.where(live, scores - top, 0.0)), 0.0)
        return scores - top - jnp.log(jnp.sum(scaled, axis=0, keepdims=True))

    log_t, log_s = log_probs(teacher), log_probs(student)
    prob_t = jnp.where(live, count * jnp.exp(jnp.where(live, log_t, 0.0)), 0.0)
    prob_s = jnp.where(live, count * jnp.exp(jnp.where(live, log_s, 0.0)), 0.0)
    loss = jnp.sum(jnp.where(live, prob_t * (log_t - log_s), 0.0), axis=0, keepdims=True)
    mine = iota((1, queries), 1) == index
    loss_ref[...] = jnp.sum(jnp.where(mine, loss, 0.0), axis=1, keepdims=True)
    own_teacher = jnp.sum(jnp.where(mine, teacher, 0.0), axis=1, keepdims=True)
    for b in range(BLOCKS):
        hit = iota((total, BLOCK), 0) == slot_ref[b : b + 1]
        score_ref[:, b * BLOCK : (b + 1) * BLOCK] = jnp.sum(jnp.where(hit, own_teacher, 0.0), axis=0, keepdims=True)
    grad = (prob_s - prob_t) * student_scale
    held[...] = grad
    own = held[pl.ds(pl.multiple_of(index * passages, passages), passages), :]
    gp_ref[...] = split_dot(own, sq_ref[...])
    rows_held[...] = grad.T
    row = rows_held[pl.ds(index, 1), :]
    gq_ref[...] = split_dot(jnp.broadcast_to(row, (8, total)), sp_ref[...])[:1]


def call(kernel, **kw):
    return pl.pallas_call(kernel, compiler_params=pltpu.CompilerParams(vmem_limit_bytes=VMEM_LIMIT), **kw)


def remote_call(kernel, number, **kw):
    params = pltpu.CompilerParams(vmem_limit_bytes=VMEM_LIMIT, collective_id=number, has_side_effects=True)
    return pl.pallas_call(kernel, compiler_params=params, **kw)


def local(n_pb, n_pa, query_kv, student_query, block_holder, cand_local, counts, passage_qkv, passage_resid, student_passage, w_o, ln_gain, ln_bias, w_dense, b_dense, w_out):
    f32, bf16 = jnp.float32, jnp.bfloat16
    axes = ("pb", "pa")
    column = lax.axis_index("pa")
    index = lax.axis_index("pb") * n_pa + column
    nq = n_pb * n_pa
    passages, _, length, width = passage_qkv.shape
    keys = query_kv.shape[2]
    rows = passages * length
    total = nq * passages
    blocks, slot_len = cand_local.shape[1:]
    slots = blocks * slot_len

    anywhere, vmem, smem = (pl.BlockSpec(memory_space=m) for m in (pl.ANY, pltpu.VMEM, pltpu.SMEM))
    value, more, kwt, part = remote_call(
        functools.partial(gather_kernel, n_pb, n_pa),
        1,
        in_specs=[anywhere, vmem, vmem, vmem, vmem, vmem, smem],
        out_specs=(anywhere, anywhere, vmem, vmem),
        out_shape=(
            jax.ShapeDtypeStruct((nq, keys, width), bf16),
            jax.ShapeDtypeStruct((nq, 16, width), bf16),
            jax.ShapeDtypeStruct((n_pa, PAIRS, 2 * passages, n_pb * keys), bf16),
            jax.ShapeDtypeStruct((n_pa, n_pb * passages, width), f32),
        ),
        scratch_shapes=[
            pltpu.VMEM((nq, keys, width), bf16),
            pltpu.VMEM((rows, width), bf16),
            pltpu.VMEM((PAIRS, 2, rows), f32),
            pltpu.VMEM((16, width), f32),
            pltpu.VMEM((16, width), bf16),
            pltpu.SemaphoreType.DMA((27, n_pa)),
            pltpu.SemaphoreType.DMA((24, n_pa)),
            pltpu.SemaphoreType.DMA((3,)),
        ],
    )(query_kv, passage_qkv, student_passage, student_query, cand_local, block_holder, counts)

    device = index.reshape(1).astype(jnp.int32)
    sp, sq, student, count, own_id = call(
        functools.partial(list_kernel, n_pa),
        in_specs=[smem, vmem],
        out_shape=(
            jax.ShapeDtypeStruct((total, width), bf16),
            jax.ShapeDtypeStruct((nq, width), bf16),
            jax.ShapeDtypeStruct((total, nq), f32),
            jax.ShapeDtypeStruct((total, nq), f32),
            jax.ShapeDtypeStruct((blocks, slot_len), jnp.int32),
        ),
    )(device, more)

    whole = lambda *shape: pl.BlockSpec(shape, lambda i: (0,) * len(shape))
    groups = 2
    step = groups * n_pb
    teacher = call(
        functools.partial(head_kernel, step, n_pa),
        grid=(n_pa // groups,),
        in_specs=[
            whole(nq, keys, width),
            pl.BlockSpec((groups, PAIRS, 2 * passages, n_pb * keys), lambda i: (i, 0, 0, 0)),
            pl.BlockSpec((groups, n_pb * passages, width), lambda i: (i, 0, 0)),
            whole(passages, width),
            whole(width, width),
            whole(1, width),
            whole(1, width),
            whole(width, width),
            whole(1, width),
            whole(1, width),
        ],
        out_specs=whole(passages, nq),
        out_shape=jax.ShapeDtypeStruct((passages, nq), f32),
        scratch_shapes=[pltpu.VMEM((step * passages, width), bf16), pltpu.VMEM((nq, passages), f32)],
    )(value, kwt, part, passage_resid, w_o, ln_gain[None], ln_bias[None], w_dense, b_dense[None], w_out[None])

    teacher_all = remote_call(
        functools.partial(share_kernel, n_pb, n_pa),
        2,
        in_specs=[vmem],
        out_specs=vmem,
        out_shape=jax.ShapeDtypeStruct((n_pb, n_pa, passages, nq), f32),
        scratch_shapes=[
            pltpu.SemaphoreType.DMA((n_pa + n_pb,)),
            pltpu.SemaphoreType.DMA((n_pa + n_pb,)),
            pltpu.SemaphoreType.DMA((1,)),
        ],
    )(teacher).reshape(total, nq)
    scores, loss, grad_query, grad_passage = call(
        loss_kernel,
        in_specs=[vmem] * 6 + [smem],
        out_shape=(
            jax.ShapeDtypeStruct((1, slots), f32),
            jax.ShapeDtypeStruct((1, 1), f32),
            jax.ShapeDtypeStruct((1, width), f32),
            jax.ShapeDtypeStruct((passages, width), f32),
        ),
        scratch_shapes=[pltpu.VMEM((total, nq), f32), pltpu.VMEM((nq, total), f32)],
    )(teacher_all, student, count, own_id, sp, sq, device)
    return scores, loss.reshape(1), grad_query, grad_passage


def solution(mesh):
    placed = (
        P(("pb", "pa"), None, None, None),
        P(("pb", "pa"), None),
        P("pb", None, None),
        P("pb", None, None),
        P("pb"),
        P(("pa", "pb"), None, None, None),
        P(("pa", "pb"), None),
        P(("pa", "pb"), None),
        P(),
        P(),
        P(),
        P(),
        P(),
        P(),
    )
    return jax.shard_map(
        functools.partial(local, mesh.shape["pb"], mesh.shape["pa"]),
        mesh=mesh,
        in_specs=placed,
        out_specs=(P(("pb", "pa"), None), P(("pb", "pa")), P(("pb", "pa"), None), P(("pa", "pb"), None)),
        check_vma=False,
    )
```

```python
import functools

import jax
import jax.numpy as jnp
from jax import lax
from jax.experimental import pallas as pl
from jax.experimental.pallas import tpu as pltpu
from jax.sharding import PartitionSpec as P

HEADS = 16
HEAD_DIM = 64
PAIRS = HEADS // 2
BLOCK = 32
BLOCKS = 2
LANES = 128
student_scale = 0.125
norm_eps = 1e-05
VMEM_LIMIT = 56 * 1024 * 1024
NT = (((1,), (1,)), ((), ()))


def iota(shape, axis):
    return lax.broadcasted_iota(jnp.int32, shape, axis)


def pair_masks(rows):
    low = iota((rows, LANES), 1) < HEAD_DIM
    return low, jnp.logical_not(low)


def attend_pair(qkv_ref, out_ref, lse_ref, k):
    passages, _, length, _ = qkv_ref.shape
    rows = passages * length
    masks = pair_masks(rows)
    same = iota((rows, rows), 0) // length == iota((rows, rows), 1) // length
    lanes = pl.ds(pl.multiple_of(k * LANES, LANES), LANES)
    q = qkv_ref[:, 0, :, lanes].reshape(rows, LANES)
    key = qkv_ref[:, 1, :, lanes].reshape(rows, LANES)
    value = qkv_ref[:, 2, :, lanes].reshape(rows, LANES)
    outs, lses = [], []
    for mask in masks:
        q_head = jnp.where(mask, q.astype(jnp.float32) * 0.125, 0.0).astype(jnp.bfloat16)
        scores = lax.dot_general(key, q_head, NT, preferred_element_type=jnp.float32)
        scores = jnp.where(same, scores, -1e30)
        top = jnp.max(scores, axis=0, keepdims=True)
        scaled = jnp.exp(scores - top)
        total = jnp.sum(scaled, axis=0, keepdims=True)
        lses.append(top + jnp.log(total))
        probs = (scaled * (1.0 / total)).T.astype(jnp.bfloat16)
        outs.append(jnp.dot(probs, value, preferred_element_type=jnp.float32))
    out_ref[:, lanes] = jnp.where(masks[0], outs[0], outs[1]).astype(jnp.bfloat16)
    lse_ref[k] = jnp.concatenate(lses, axis=0)


def gather_kernel(
    n_pb, n_pa, kv_ref, qkv_ref, sp_ref, sq_ref, cand_ref, holder_ref, count_ref,
    vals_ref, more_ref, kwt_ref, part_ref, got_ref, out_ref, lse_ref, wide, packed, send, recv, here,
):
    me_b, me_a = lax.axis_index("pb"), lax.axis_index("pa")
    core = me_b % 2
    spot = me_b // 2
    sx, sy = spot % 2, spot // 2
    beside = (sy * 2 + 1 - sx) * 2 + core
    across = ((1 - sy) * 2 + sx) * 2 + core
    corner = ((1 - sy) * 2 + 1 - sx) * 2 + core
    other = spot * 2 + 1 - core
    bufs = (got_ref, vals_ref, more_ref)
    pieces = range(3)
    mesh_ids = pl.DeviceIdType.MESH

    def copy(kind, piece, owner_a, owner_b, to_b, to_a, landing=None):
        ref = bufs[piece].at[owner_b * n_pa + owner_a]
        landing = kind if landing is None else landing
        return pltpu.make_async_remote_copy(
            src_ref=ref,
            dst_ref=ref,
            send_sem=send.at[kind * 3 + piece, owner_a],
            recv_sem=recv.at[landing * 3 + piece, owner_a],
            device_id=(to_b, to_a),
            device_id_type=mesh_ids,
        )

    def up(piece, owner_a):
        return copy(0, piece, owner_a, me_b, me_b, me_a + 1)

    def down(piece, owner_a):
        return copy(8, piece, owner_a, me_b, me_b, me_a - 1, landing=0)

    def arrived(kind, piece, owner_a, owner_b):
        copy(kind, piece, owner_a, owner_b, other, me_a).wait_recv()

    barrier = pltpu.get_barrier_semaphore()
    for peer in (beside, across, other):
        pl.semaphore_signal(barrier, inc=1, device_id=(peer, me_a), device_id_type=mesh_ids)

    @pl.when(me_a + 1 < n_pa)
    def _():
        pl.semaphore_signal(barrier, inc=1, device_id=(me_b, me_a + 1), device_id_type=mesh_ids)

    @pl.when(me_a > 0)
    def _():
        pl.semaphore_signal(barrier, inc=1, device_id=(me_b, me_a - 1), device_id_type=mesh_ids)

    passages = sp_ref.shape[0]
    width = sp_ref.shape[1]
    mine = me_b * n_pa + me_a
    own_copies = [
        pltpu.make_async_copy(kv_ref.at[0, 0], got_ref.at[mine], here.at[0]),
        pltpu.make_async_copy(kv_ref.at[0, 1], vals_ref.at[mine], here.at[1]),
        pltpu.make_async_copy(packed, more_ref.at[mine], here.at[2]),
    ]
    own_copies[0].start()
    own_copies[1].start()
    wide[...] = jnp.zeros_like(wide)
    wide[:passages] = sp_ref[...].astype(jnp.float32)
    wide[passages : passages + 1] = sq_ref[...].astype(jnp.float32)
    wide[passages + 1 : passages + 2] = jnp.full((1, width), count_ref[me_a].astype(jnp.float32))
    wide[passages + 2 : passages + 2 + BLOCKS, :BLOCK] = cand_ref[me_a].astype(jnp.float32)
    wide[passages + 2 + BLOCKS : passages + 2 + 2 * BLOCKS] = jnp.broadcast_to(
        holder_ref[me_a].astype(jnp.float32), (BLOCKS, width)
    )
    packed[...] = wide[...].astype(jnp.bfloat16)
    own_copies[2].start()
    for one in own_copies:
        one.wait()

    @pl.when((me_a > 0) & (me_a + 1 < n_pa))
    def _():
        pl.semaphore_wait(barrier, 5)

    @pl.when((me_a == 0) | (me_a + 1 == n_pa))
    def _():
        pl.semaphore_wait(barrier, 4)

    def column(owner, fresh):
        if not fresh:
            for piece in pieces:
                arrived(0, piece, owner, me_b)

        @pl.when((owner <= me_a) & (me_a + 1 < n_pa))
        def _():
            for piece in pieces:
                up(piece, owner).start()

        @pl.when((owner >= me_a) & (me_a > 0))
        def _():
            for piece in pieces:
                down(piece, owner).start()

        for piece in pieces:
            copy(1, piece, owner, me_b, beside, me_a).start()
            copy(2, piece, owner, me_b, across, me_a).start()
        for piece in pieces:
            copy(4, piece, owner, me_b, other, me_a).start()

    def forward(owner):
        for piece in pieces:
            near, kind = (across, 2) if piece == 1 else (beside, 1)
            arrived(kind, piece, owner, near)
            copy(3, piece, owner, near, beside if piece == 1 else across, me_a).start()
            copy(6 if piece == 1 else 5, piece, owner, near, other, me_a).start()
        for piece in pieces:
            near, kind = (beside, 1) if piece == 1 else (across, 2)
            arrived(kind, piece, owner, near)
            copy(5 if piece == 1 else 6, piece, owner, near, other, me_a).start()

    def last(owner):
        for piece in pieces:
            arrived(3, piece, owner, corner)
            copy(7, piece, owner, corner, other, me_a).start()

    def both(distance, act):
        for owner in (me_a - distance, me_a + distance):
            @pl.when((owner >= 0) & (owner < n_pa))
            def _(owner=owner):
                act(owner)

    def stage(distance, carry):
        @pl.when(distance < n_pa)
        def _():
            both(distance, lambda owner: column(owner, False))

        @pl.when(distance == 1)
        def _():
            forward(me_a)

        @pl.when((distance > 1) & (distance <= n_pa))
        def _():
            both(distance - 1, forward)

        @pl.when(distance == 2)
        def _():
            last(me_a)

        @pl.when((distance > 2) & (distance <= n_pa + 1))
        def _():
            both(distance - 2, last)

        @pl.when(distance < 3)
        def _():
            for half in range(2):
                attend_pair(qkv_ref, out_ref, lse_ref, 2 + distance * 2 + half)

        def score(side, inner):
            owner = me_a + (2 * side - 1) * (distance - 2)

            @pl.when((owner >= 0) & (owner < n_pa) & ((distance > 2) | (side > 0)))
            def _():
                for kind, near in ((4, me_b), (5, beside), (6, across), (7, corner)):
                    arrived(kind, 0, owner, near + 1 - 2 * core)
                cross_group(got_ref, qkv_ref, out_ref, lse_ref, kwt_ref, part_ref, owner, n_pb, n_pa)

            return inner

        @pl.when(distance > 1)
        def _():
            lax.fori_loop(0, 2, score, 0)

        return carry

    def finish(owner, carry):
        for piece in pieces:
            for kind, near in ((4, me_b), (5, beside), (6, across), (7, corner)):
                if piece > 0:
                    arrived(kind, piece, owner, near + 1 - 2 * core)
                copy(kind, piece, owner, near, other, me_a).wait_send()
            copy(1, piece, owner, me_b, beside, me_a).wait_send()
            copy(2, piece, owner, me_b, across, me_a).wait_send()
            if piece == 1:
                copy(3, piece, owner, across, beside, me_a).wait_send()
            else:
                copy(3, piece, owner, beside, across, me_a).wait_send()

        @pl.when((owner <= me_a) & (me_a + 1 < n_pa))
        def _():
            for piece in pieces:
                up(piece, owner).wait_send()

        @pl.when((owner >= me_a) & (me_a > 0))
        def _():
            for piece in pieces:
                down(piece, owner).wait_send()

        return carry

    column(me_a, True)
    for half in range(4):
        attend_pair(qkv_ref, out_ref, lse_ref, half)
    lax.fori_loop(1, n_pa + 2, stage, 0)
    lax.fori_loop(0, n_pa, finish, 0)


def share_kernel(
    n_pb, n_pa, own_ref, extra_ref, all_ref, sp_ref, sq_ref, student_ref, count_ref, slot_ref, send, recv, here
):
    me_b, me_a = lax.axis_index("pb"), lax.axis_index("pa")
    mesh_ids = pl.DeviceIdType.MESH

    def column(step, from_a):
        return pltpu.make_async_remote_copy(
            src_ref=own_ref,
            dst_ref=all_ref.at[me_b, from_a],
            send_sem=send.at[step],
            recv_sem=recv.at[step],
            device_id=(me_b, (me_a + step) % n_pa),
            device_id_type=mesh_ids,
        )

    def plane(step, from_b):
        return pltpu.make_async_remote_copy(
            src_ref=all_ref.at[from_b],
            dst_ref=all_ref.at[from_b],
            send_sem=send.at[n_pa + step],
            recv_sem=recv.at[n_pa + step],
            device_id=((me_b + step) % n_pb, me_a),
            device_id_type=mesh_ids,
        )

    def loop(first, last, act):
        def one(step, carry):
            act(step)
            return carry

        lax.fori_loop(first, last, one, 0)

    barrier = pltpu.get_barrier_semaphore()

    def greet_column(step):
        pl.semaphore_signal(barrier, inc=1, device_id=(me_b, (me_a + step) % n_pa), device_id_type=mesh_ids)

    def greet_plane(step):
        pl.semaphore_signal(barrier, inc=1, device_id=((me_b + step) % n_pb, me_a), device_id_type=mesh_ids)

    loop(1, n_pa, greet_column)
    loop(1, n_pb, greet_plane)
    own_copy = pltpu.make_async_copy(own_ref, all_ref.at[me_b, me_a], here.at[0])
    own_copy.start()
    pl.semaphore_wait(barrier, n_pa + n_pb - 2)
    loop(1, n_pa, lambda step: column(step, me_a).start())
    own_copy.wait()
    loop(1, n_pa, lambda step: column(step, (me_a + n_pa - step) % n_pa).wait_recv())
    loop(1, n_pb, lambda step: plane(step, me_b).start())
    list_slots(n_pa, me_b * n_pa + me_a, extra_ref, sp_ref, sq_ref, student_ref, count_ref, slot_ref)
    loop(1, n_pb, lambda step: plane(step, (me_b + n_pb - step) % n_pb).wait_recv())
    loop(1, n_pa, lambda step: column(step, me_a).wait_send())
    loop(1, n_pb, lambda step: plane(step, me_b).wait_send())


def list_slots(n_pa, index, extra_ref, sp_ref, sq_ref, student_ref, count_ref, slot_ref):
    queries, _, width = extra_ref.shape
    total = sp_ref.shape[0]
    passages = total // queries
    extra = extra_ref[...].astype(jnp.float32)
    sp = extra[:, :passages].reshape(total, width).astype(jnp.bfloat16)
    rest = extra[:, passages:]
    sq = rest[:, 0].astype(jnp.bfloat16)
    sp_ref[...] = sp
    sq_ref[...] = sq
    student_ref[...] = student_scale * lax.dot_general(sp, sq, NT, preferred_element_type=jnp.float32)
    real = rest[:, 1, :LANES].T[:1]
    ids = [rest[:, 2 + b, :LANES].T for b in range(BLOCKS)]
    holders = [rest[:, 2 + BLOCKS + b, :LANES].T[:1] for b in range(BLOCKS)]
    own_rest = extra_ref[pl.ds(index, 1)].astype(jnp.float32)[0, passages:]
    slot = own_rest[2 : 2 + BLOCKS, :BLOCK]
    slot_group = jnp.floor(slot / passages)
    slot_id = (slot_group * n_pa + own_rest[2 + BLOCKS : 2 + 2 * BLOCKS, :BLOCK]) * passages + slot - slot_group * passages
    number_of = (iota((BLOCKS, BLOCK), 0) * BLOCK + iota((BLOCKS, BLOCK), 1)).astype(jnp.float32)
    slot_ref[...] = jnp.where(number_of < own_rest[1:2, :BLOCK], slot_id, -1.0).astype(jnp.int32)
    row = iota((total, queries), 0).astype(jnp.float32)
    number = jnp.floor(row / passages)
    part = row - number * passages
    group = jnp.floor(number / n_pa)
    holder_of = number - group * n_pa
    local_of = group * passages + part
    count = jnp.zeros((total, queries), jnp.float32)
    for b in range(BLOCKS):
        tally = jnp.zeros((total, queries), jnp.float32)
        for c in range(BLOCK):
            name = jnp.where(real > b * BLOCK + c, ids[b][c : c + 1], -1.0)
            tally = tally + (local_of == name).astype(jnp.float32)
        count = count + jnp.where(holder_of == holders[b], tally, 0.0)
    count_ref[...] = count


def cross_group(k_ref, q_ref, so_ref, lse_ref, kwt_ref, part_ref, owner, n_pb, n_pa):
    keys = k_ref.shape[1]
    passages, _, length, _ = q_ref.shape
    rows = passages * length
    masks = pair_masks(rows)
    out_low = iota((n_pb * passages, LANES), 1) < HEAD_DIM
    own = (iota((passages, rows), 1) // length == iota((passages, rows), 0)).astype(jnp.float32)
    spots = [
        jnp.where(iota((rows, LANES), 1) == iota((rows, LANES), 0) // length + h * passages, 1.0 / length, 0.0).astype(
            jnp.bfloat16
        )
        for h in range(2)
    ]

    def body(k, carry):
        lanes = pl.ds(pl.multiple_of(k * LANES, LANES), LANES)
        q = q_ref[:, 0, :, lanes].reshape(rows, LANES)
        key = jnp.concatenate([k_ref[i * n_pa + owner, :, lanes] for i in range(n_pb)], axis=0)
        so = so_ref[:, lanes]
        lse = lse_ref[k]
        weights, parts = None, []
        for h in range(2):
            q_head = jnp.where(masks[h], q.astype(jnp.float32) * 0.125, 0.0).astype(jnp.bfloat16)
            scores = lax.dot_general(key, q_head, NT, preferred_element_type=jnp.float32)
            scores = scores.reshape(n_pb, keys, rows)
            self_lse = lse[h : h + 1]
            top = jnp.maximum(jnp.max(scores, axis=1), self_lse)
            scaled = jnp.exp(scores - top[:, None, :])
            self_term = jnp.exp(self_lse - top)
            inverse = 1.0 / (jnp.sum(scaled, axis=1) + self_term)
            spread = (scaled * inverse[:, None, :]).reshape(n_pb * keys, rows).astype(jnp.bfloat16)
            weight = jnp.dot(spread, spots[h], preferred_element_type=jnp.float32)
            weights = weight if weights is None else weights + weight
            token = self_term * inverse * (1.0 / length)
            token = (token[:, None, :] * own[None]).reshape(n_pb * passages, rows).astype(jnp.bfloat16)
            parts.append(jnp.dot(token, so, preferred_element_type=jnp.float32))
        part_ref[owner, :, lanes] = jnp.where(out_low, parts[0], parts[1])
        kwt_ref[owner, k] = weights.T[: 2 * passages].astype(jnp.bfloat16)
        return carry

    lax.fori_loop(0, PAIRS, body, 0, unroll=4)


def head_kernel(queries, n_pa, v_ref, kwt_ref, part_ref, resid_ref, wo_ref, gain_ref, bias_ref, wd_ref, bd_ref, out_w_ref, teacher_ref, pooled, table):
    step = pl.program_id(0)
    _, keys, width = v_ref.shape
    passages = resid_ref.shape[0]
    groups, _, _, cols = kwt_ref.shape
    group = cols // keys
    span = 2 * passages
    own = (iota((group, span, cols), 2) // keys == iota((group, span, cols), 0)).astype(jnp.float32)
    low = iota((group, passages, LANES), 2) < HEAD_DIM

    def body(k, carry):
        lanes = pl.ds(pl.multiple_of(k * LANES, LANES), LANES)
        for c in range(groups):
            weight = kwt_ref[c, k].astype(jnp.float32)
            weight = (weight[None] * own).reshape(group * span, cols).astype(jnp.bfloat16)
            value = jnp.concatenate(
                [v_ref[i * n_pa + step * groups + c, :, lanes] for i in range(group)], axis=0
            )
            got = jnp.dot(weight, value, preferred_element_type=jnp.float32)
            got = got.reshape(group, 2, passages, LANES)
            got = jnp.where(low, got[:, 0], got[:, 1]).reshape(group * passages, LANES)
            rows = slice(c * group * passages, (c + 1) * group * passages)
            pooled[rows, lanes] = (got + part_ref[c, :, lanes]).astype(jnp.bfloat16)
        return carry

    @pl.when(step == 0)
    def _():
        table[...] = jnp.zeros_like(table)

    @pl.when(step >= 0)
    def _():
        lax.fori_loop(0, PAIRS, body, 0, unroll=4)
        mixed = jnp.dot(pooled[...], wo_ref[...], preferred_element_type=jnp.float32)
        mixed = (mixed.reshape(queries, passages, width) + resid_ref[...].astype(jnp.float32)[None]).reshape(
            queries * passages, width
        )
        mean = jnp.mean(mixed, axis=-1, keepdims=True)
        centered = mixed - mean
        var = jnp.mean(centered * centered, axis=-1, keepdims=True)
        normed = (centered * lax.rsqrt(var + norm_eps) * gain_ref[...] + bias_ref[...]).astype(jnp.bfloat16)
        hidden = jnp.tanh(jnp.dot(normed, wd_ref[...], preferred_element_type=jnp.float32) + bd_ref[...])
        score = jnp.sum((hidden * out_w_ref[...]).reshape(queries, passages, width), axis=-1)
        for i in range(queries):
            table[pl.ds(i % group * n_pa + step * groups + i // group, 1), :] = score[i : i + 1]

    @pl.when(step == pl.num_programs(0) - 1)
    def _():
        teacher_ref[...] = table[...].T


def split_dot(a, b):
    high = a.astype(jnp.bfloat16)
    low = (a - high.astype(jnp.float32)).astype(jnp.bfloat16)
    return jnp.dot(high, b, preferred_element_type=jnp.float32) + jnp.dot(low, b, preferred_element_type=jnp.float32)


def loss_kernel(teacher_ref, student_ref, count_ref, slot_ref, sp_ref, sq_ref, index_ref, score_ref, loss_ref, gq_ref, gp_ref, held, rows_held):
    teacher, student, count = teacher_ref[...], student_ref[...], count_ref[...]
    total, queries = teacher.shape
    passages = gp_ref.shape[0]
    index = index_ref[0]
    live = count > 0.0

    def log_probs(scores):
        top = jnp.max(jnp.where(live, scores, -1e30), axis=0, keepdims=True)
        scaled = jnp.where(live, count * jnp.exp(jnp.where(live, scores - top, 0.0)), 0.0)
        return scores - top - jnp.log(jnp.sum(scaled, axis=0, keepdims=True))

    log_t, log_s = log_probs(teacher), log_probs(student)
    prob_t = jnp.where(live, count * jnp.exp(jnp.where(live, log_t, 0.0)), 0.0)
    prob_s = jnp.where(live, count * jnp.exp(jnp.where(live, log_s, 0.0)), 0.0)
    loss = jnp.sum(jnp.where(live, prob_t * (log_t - log_s), 0.0), axis=0, keepdims=True)
    mine = iota((1, queries), 1) == index
    loss_ref[...] = jnp.sum(jnp.where(mine, loss, 0.0), axis=1, keepdims=True)
    own_teacher = jnp.sum(jnp.where(mine, teacher, 0.0), axis=1, keepdims=True)
    for b in range(BLOCKS):
        hit = iota((total, BLOCK), 0) == slot_ref[b : b + 1]
        score_ref[:, b * BLOCK : (b + 1) * BLOCK] = jnp.sum(jnp.where(hit, own_teacher, 0.0), axis=0, keepdims=True)
    grad = (prob_s - prob_t) * student_scale
    held[...] = grad
    own = held[pl.ds(pl.multiple_of(index * passages, passages), passages), :]
    gp_ref[...] = split_dot(own, sq_ref[...])
    rows_held[...] = grad.T
    row = rows_held[pl.ds(index, 1), :]
    gq_ref[...] = split_dot(jnp.broadcast_to(row, (8, total)), sp_ref[...])[:1]


def call(kernel, **kw):
    return pl.pallas_call(kernel, compiler_params=pltpu.CompilerParams(vmem_limit_bytes=VMEM_LIMIT), **kw)


def remote_call(kernel, number, **kw):
    params = pltpu.CompilerParams(vmem_limit_bytes=VMEM_LIMIT, collective_id=number, has_side_effects=True)
    return pl.pallas_call(kernel, compiler_params=params, **kw)


def local(n_pb, n_pa, query_kv, student_query, block_holder, cand_local, counts, passage_qkv, passage_resid, student_passage, w_o, ln_gain, ln_bias, w_dense, b_dense, w_out):
    f32, bf16 = jnp.float32, jnp.bfloat16
    axes = ("pb", "pa")
    column = lax.axis_index("pa")
    index = lax.axis_index("pb") * n_pa + column
    nq = n_pb * n_pa
    passages, _, length, width = passage_qkv.shape
    keys = query_kv.shape[2]
    rows = passages * length
    total = nq * passages
    blocks, slot_len = cand_local.shape[1:]
    slots = blocks * slot_len

    anywhere, vmem, smem = (pl.BlockSpec(memory_space=m) for m in (pl.ANY, pltpu.VMEM, pltpu.SMEM))
    value, more, kwt, part = remote_call(
        functools.partial(gather_kernel, n_pb, n_pa),
        1,
        in_specs=[anywhere, vmem, vmem, vmem, vmem, vmem, smem],
        out_specs=(anywhere, anywhere, vmem, vmem),
        out_shape=(
            jax.ShapeDtypeStruct((nq, keys, width), bf16),
            jax.ShapeDtypeStruct((nq, 16, width), bf16),
            jax.ShapeDtypeStruct((n_pa, PAIRS, 2 * passages, n_pb * keys), bf16),
            jax.ShapeDtypeStruct((n_pa, n_pb * passages, width), f32),
        ),
        scratch_shapes=[
            pltpu.VMEM((nq, keys, width), bf16),
            pltpu.VMEM((rows, width), bf16),
            pltpu.VMEM((PAIRS, 2, rows), f32),
            pltpu.VMEM((16, width), f32),
            pltpu.VMEM((16, width), bf16),
            pltpu.SemaphoreType.DMA((27, n_pa)),
            pltpu.SemaphoreType.DMA((24, n_pa)),
            pltpu.SemaphoreType.DMA((3,)),
        ],
    )(query_kv, passage_qkv, student_passage, student_query, cand_local, block_holder, counts)

    device = index.reshape(1).astype(jnp.int32)
    whole = lambda *shape: pl.BlockSpec(shape, lambda i: (0,) * len(shape))
    groups = 2
    step = groups * n_pb
    teacher = call(
        functools.partial(head_kernel, step, n_pa),
        grid=(n_pa // groups,),
        in_specs=[
            whole(nq, keys, width),
            pl.BlockSpec((groups, PAIRS, 2 * passages, n_pb * keys), lambda i: (i, 0, 0, 0)),
            pl.BlockSpec((groups, n_pb * passages, width), lambda i: (i, 0, 0)),
            whole(passages, width),
            whole(width, width),
            whole(1, width),
            whole(1, width),
            whole(width, width),
            whole(1, width),
            whole(1, width),
        ],
        out_specs=whole(passages, nq),
        out_shape=jax.ShapeDtypeStruct((passages, nq), f32),
        scratch_shapes=[pltpu.VMEM((step * passages, width), bf16), pltpu.VMEM((nq, passages), f32)],
    )(value, kwt, part, passage_resid, w_o, ln_gain[None], ln_bias[None], w_dense, b_dense[None], w_out[None])

    teacher_all, sp, sq, student, count, own_id = remote_call(
        functools.partial(share_kernel, n_pb, n_pa),
        2,
        in_specs=[vmem] * 2,
        out_specs=(vmem,) * 6,
        out_shape=(
            jax.ShapeDtypeStruct((n_pb, n_pa, passages, nq), f32),
            jax.ShapeDtypeStruct((total, width), bf16),
            jax.ShapeDtypeStruct((nq, width), bf16),
            jax.ShapeDtypeStruct((total, nq), f32),
            jax.ShapeDtypeStruct((total, nq), f32),
            jax.ShapeDtypeStruct((blocks, slot_len), jnp.int32),
        ),
        scratch_shapes=[
            pltpu.SemaphoreType.DMA((n_pa + n_pb,)),
            pltpu.SemaphoreType.DMA((n_pa + n_pb,)),
            pltpu.SemaphoreType.DMA((1,)),
        ],
    )(teacher, more)
    teacher_all = teacher_all.reshape(total, nq)
    scores, loss, grad_query, grad_passage = call(
        loss_kernel,
        in_specs=[vmem] * 6 + [smem],
        out_shape=(
            jax.ShapeDtypeStruct((1, slots), f32),
            jax.ShapeDtypeStruct((1, 1), f32),
            jax.ShapeDtypeStruct((1, width), f32),
            jax.ShapeDtypeStruct((passages, width), f32),
        ),
        scratch_shapes=[pltpu.VMEM((total, nq), f32), pltpu.VMEM((nq, total), f32)],
    )(teacher_all, student, count, own_id, sp, sq, device)
    return scores, loss.reshape(1), grad_query, grad_passage


def solution(mesh):
    placed = (
        P(("pb", "pa"), None, None, None),
        P(("pb", "pa"), None),
        P("pb", None, None),
        P("pb", None, None),
        P("pb"),
        P(("pa", "pb"), None, None, None),
        P(("pa", "pb"), None),
        P(("pa", "pb"), None),
        P(),
        P(),
        P(),
        P(),
        P(),
        P(),
    )
    return jax.shard_map(
        functools.partial(local, mesh.shape["pb"], mesh.shape["pa"]),
        mesh=mesh,
        in_specs=placed,
        out_specs=(P(("pb", "pa"), None), P(("pb", "pa")), P(("pb", "pa"), None), P(("pa", "pb"), None)),
        check_vma=False,
    )
```
